32 devices in a mesh: row: 4 (over y, x), col: 8 (over z, core).
Axes of the slice: x: 2, y: 2, z: 4, core: 2. Of those that a mesh axis runs over, the one named last changes fastest.
Arguments:
- tokens: bfloat16 [512, 6144], P('row', 'col'), may hold values from -6 to 6
- w_query: bfloat16 [6144, 1024], P('row', 'col'), may hold values from -0.078125 to 0.078125
- w_key: bfloat16 [6144, 1024], P('row', 'col'), may hold values from -0.078125 to 0.078125
- w_value: bfloat16 [6144, 1024], P('row', 'col'), may hold values from -0.078125 to 0.078125
- w_out: bfloat16 [1024, 6144], P('row', 'col'), may hold values from -0.1875 to 0.1875
- key_cache: bfloat16 [8192, 1024], P('row', 'col'), may hold values from -6 to 6
- value_cache: bfloat16 [8192, 1024], P('row', 'col'), may hold values from -6 to 6
- query_gain: float32 [128], replicated, may hold values from 1 to 2.5
- key_gain: float32 [128], replicated, may hold values from 1 to 2.5
- out_gate: float32 [6144], P('col'), may hold values from 0.5 to 2
- cotangent: bfloat16 [512, 6144], P('row', 'col'), may hold values from -6 to 6
Outputs:
- layer_out: bfloat16 [512, 6144], P('row', 'col')
- attention_cotangent: bfloat16 [512, 1024], P('row', 'col')
The draws below stay inside these ranges and needn't reach their ends.
All inputs are finite; a program needn't handle non-finite values.
Results may differ from the reference program's by a relative error of at most 0.012.
Values may be sent and summed in bfloat16 or wider, within the bound.
No kernel may reach another device: no remote copies, remote signals or barrier semaphores. Data moves between devices by JAX's collectives and lax.ppermute only.
A program may use at most 64 MiB of HBM per device.

```python
import math
import jax
import jax.numpy as jnp
from jax import lax

D = 6144
HEAD_DIM = 128
HEADS = 8
FA = 1024
TOKENS = 512
CACHE = 8192


def levels(stream_key, dims, shards, smallest, high):
    loudness = 1.0
    for dim, shards_of in shards:
        heights = jax.random.uniform(jax.random.fold_in(jax.random.fold_in(stream_key, 6), dim), (shards_of,), jnp.float32, smallest / len(shards), high / len(shards))
        loudness = loudness * jnp.repeat(jnp.exp(heights), dims[dim] // shards_of).reshape((-1,) + (1,) * (len(dims) - 1 - dim))
    return loudness


def bell_draw(rng, dims, spread, limit, cuts=(), held_as=jnp.bfloat16):
    array = spread * jax.random.normal(rng, dims, jnp.float32)
    if cuts:
        array = array * levels(rng, dims, cuts, -0.22, 0.18)
    return jnp.clip(array, -limit, limit).astype(held_as)


def setup_inputs(seed: int = 0) -> dict:
    key_of = jax.random.split(jax.random.key(seed), 12)
    return {
        "tokens": bell_draw(key_of[0], (TOKENS, D), 1.0, 6.0, ((0, 4), (1, 8))),
        "w_query": bell_draw(key_of[1], (D, FA), D ** -0.5, 0.078125, ((0, 4), (1, 8))),
        "w_key": bell_draw(key_of[2], (D, FA), D ** -0.5, 0.078125, ((0, 4), (1, 8))),
        "w_value": bell_draw(key_of[3], (D, FA), D ** -0.5, 0.078125, ((0, 4), (1, 8))),
        "w_out": bell_draw(key_of[4], (FA, D), FA ** -0.5, 0.1875, ((0, 4), (1, 8))),
        "key_cache": bell_draw(key_of[5], (CACHE, FA), 1.0, 6.0, ((0, 4), (1, 8))),
        "value_cache": bell_draw(key_of[6], (CACHE, FA), 1.0, 6.0, ((0, 4), (1, 8))),
        "query_gain": jnp.clip(jnp.exp(jax.random.uniform(key_of[7], (HEAD_DIM,), jnp.float32, math.log(1.0), math.log(2.5))), 1.0, 2.5),
        "key_gain": jnp.clip(jnp.exp(jax.random.uniform(key_of[8], (HEAD_DIM,), jnp.float32, math.log(1.0), math.log(2.5))), 1.0, 2.5),
        "out_gate": jnp.clip(jnp.exp(math.log(2.0) - 1.3862944 * jax.random.uniform(key_of[9], (D,), jnp.float32) ** levels(key_of[9], (D,), ((0, 8),), -0.2, 0.2)), 0.5, 2.0),
        "cotangent": bell_draw(key_of[10], (TOKENS, D), 1.0, 6.0, ((0, 4), (1, 8))),
    }


epsilon = 1e-06

def norm_heads(values, gain):
    wide = values.astype(jnp.float32)
    mean_square = lax.optimization_barrier(jnp.mean(wide * wide, axis=-1, keepdims=True))
    return (wide * lax.rsqrt(mean_square + epsilon) * gain.astype(jnp.float32)).astype(jnp.bfloat16)

def reference(tokens, w_query, w_key, w_value, w_out, key_cache, value_cache, query_gain, key_gain, out_gate, cotangent):
    query = jnp.dot(tokens, w_query, preferred_element_type=jnp.float32).astype(jnp.bfloat16)
    key_new = jnp.dot(tokens, w_key, preferred_element_type=jnp.float32).astype(jnp.bfloat16)
    value_new = jnp.dot(tokens, w_value, preferred_element_type=jnp.float32).astype(jnp.bfloat16)
    slab_rows = query.shape[0]
    query_norm = norm_heads(query.reshape(slab_rows, HEADS, HEAD_DIM), query_gain)
    key_all = jnp.concatenate([key_cache, key_new], axis=0)
    key_norm = norm_heads(key_all.reshape(-1, HEADS, HEAD_DIM), key_gain)
    value_all = jnp.concatenate([value_cache, value_new], axis=0).reshape(-1, HEADS, HEAD_DIM)
    scale = HEAD_DIM ** (-0.5)

    def one_head(operands):
        query_head, key_head, value_head = operands
        scores = jnp.dot(query_head.astype(jnp.float32), key_head.astype(jnp.float32).T) * scale
        weights = jnp.exp(scores)
        totals = lax.optimization_barrier(jnp.sum(weights, axis=1, keepdims=True))
        weights_low = lax.optimization_barrier(weights.astype(jnp.bfloat16))
        numerators = jnp.dot(weights_low.astype(jnp.float32), value_head.astype(jnp.float32))
        return (numerators / totals).astype(jnp.bfloat16)
    per_head = lax.map(one_head, (query_norm.transpose(1, 0, 2), key_norm.transpose(1, 0, 2), value_all.transpose(1, 0, 2)))
    attention = per_head.transpose(1, 0, 2).reshape(slab_rows, HEADS * HEAD_DIM)
    branch = jnp.dot(attention, w_out, preferred_element_type=jnp.float32)
    layer_out = (tokens.astype(jnp.float32) + out_gate.astype(jnp.float32) * branch).astype(jnp.bfloat16)
    scaled = (cotangent.astype(jnp.float32) * out_gate.astype(jnp.float32)).astype(jnp.bfloat16)
    attention_cotangent = jnp.dot(scaled, w_out.T, preferred_element_type=jnp.float32).astype(jnp.bfloat16)
    return (layer_out, attention_cotangent)
```

```python
import math

import jax
import jax.numpy as jnp
from jax import lax
from jax.experimental import pallas as pl
from jax.experimental.pallas import tpu as pltpu
from jax.sharding import PartitionSpec as P

epsilon = 1e-06
both = ("row", "col")
f32 = jnp.float32
bf16 = jnp.bfloat16
tail = 16


def size_of(arrays):
    return sum(math.prod(a.shape) * jnp.dtype(a.dtype).itemsize for a in arrays)


def call(kernel, name, operands, outs, scratch=(), flops=0):
    moved = size_of(operands) + size_of(outs)
    held = moved + sum(math.prod(s.shape) * jnp.dtype(s.dtype).itemsize for s in scratch)
    whole = pl.BlockSpec(memory_space=pltpu.VMEM)
    return pl.pallas_call(
        kernel,
        out_shape=list(outs),
        in_specs=[whole] * len(operands),
        out_specs=[whole] * len(outs),
        scratch_shapes=list(scratch),
        compiler_params=pltpu.CompilerParams(vmem_limit_bytes=2 * held + (12 << 20)),
        cost_estimate=pl.CostEstimate(flops=flops, bytes_accessed=moved, transcendentals=0),
        name=name,
    )(*operands)


def dot(a, b):
    return jnp.dot(a, b, preferred_element_type=f32)


def dot_last(a, b):
    return lax.dot_general(a, b, (((1,), (1,)), ((), ())), preferred_element_type=f32)


def normed(wide, gain):
    mean_square = jnp.mean(wide * wide, axis=-1, keepdims=True)
    return wide * lax.rsqrt(mean_square + epsilon) * gain


def solution(mesh):
    R, C = mesh.shape["row"], mesh.shape["col"]
    k = C // R
    assert C == R * k and k == 2 and R & (R - 1) == 0

    def here():
        f, c = lax.axis_index("row"), lax.axis_index("col")
        return f, c // k, c % k

    def route(to):
        return [
            (r * C + z * k + q, (lambda a, b, e: a * C + b * k + e)(*to(r, z, q)))
            for r in range(R)
            for z in range(R)
            for q in range(k)
        ]

    def across_chip(x):
        return lax.ppermute(x, both, route(lambda r, z, q: (r, z, q ^ 1)))

    def over_row(x, s):
        return lax.ppermute(x, both, route(lambda r, z, q: (r ^ s, z, q)))

    def over_z(x, m):
        return lax.ppermute(x, both, route(lambda r, z, q: (r, z ^ m, q)))

    def turned(x, d):
        return lax.ppermute(x, both, route(lambda r, z, q: (z, r ^ d, q)))

    def body(
        tokens,
        w_query,
        w_key,
        w_value,
        w_out,
        key_cache,
        value_cache,
        query_gain,
        key_gain,
        out_gate,
        cotangent,
    ):
        T, F = tokens.shape
        H = query_gain.shape[0]
        cached = key_cache.shape[0]
        wide_out = w_out.shape[1]
        assert w_query.shape == (k * F, H) and w_out.shape == (k * H, wide_out) and T == H
        query_gain = query_gain.reshape(1, H)
        key_gain = key_gain.reshape(1, H)
        out_gate = out_gate.reshape(1, wide_out)
        fold = H ** (-0.5) * math.log2(math.e)

        mine = [turned(tokens, d) for d in range(R)]
        other = [across_chip(x) for x in mine]
        out_rows = [w_out] + [over_row(w_out, s) for s in range(1, R)]

        def prepare(key_ref, value_ref, gain_ref, key_out, value_out):
            key = normed(key_ref[...].astype(f32), gain_ref[...])
            key_out[...] = key.T.astype(bf16)
            value_out[:, :H] = value_ref[...]
            value_out[:, H:] = jnp.ones((cached, H), bf16)

        keys_t, values_one = call(
            prepare,
            "cache",
            (key_cache, value_cache, key_gain),
            [
                jax.ShapeDtypeStruct((H, cached), bf16),
                jax.ShapeDtypeStruct((cached, 2 * H), bf16),
            ],
        )

        def project(*refs):
            mine_refs, other_refs = refs[:R], refs[R : 2 * R]
            wq, wk, wv = refs[2 * R : 2 * R + 3]
            outs = refs[2 * R + 3 : 3 * R + 3]
            held = refs[3 * R + 3]
            f, _, q = here()
            first = pl.ds(pl.multiple_of(q * F, F), F)
            second = pl.ds(pl.multiple_of((1 - q) * F, F), F)
            w_mine = jnp.concatenate([wq[first], wk[first], wv[first]], axis=1)
            w_other = jnp.concatenate([wq[second], wk[second], wv[second]], axis=1)
            for d in range(R):
                part = (dot(mine_refs[d][...], w_mine) + dot(other_refs[d][...], w_other)).astype(bf16)
                for s in range(R):
                    outs[s][d * T : (d + 1) * T, :] = part[:, :H]
                held[d, :T] = part[:, H : 2 * H]
                held[d, T:] = part[:, 2 * H :]
            for s in range(R):
                outs[s][R * T :, :] = held[f ^ s]

        parts = call(
            project,
            "project",
            (*mine, *other, w_query, w_key, w_value),
            [jax.ShapeDtypeStruct(((R + 2) * T, H), bf16)] * R,
            [pltpu.VMEM((R, 2 * T, H), bf16)],
            flops=2 * R * T * k * F * 3 * H,
        )
        parts = [parts[0]] + [over_row(parts[s], s) for s in range(1, R)]

        def attend(*refs):
            part_refs = refs[:R]
            keys_ref, values_ref, query_gain_ref, key_gain_ref = refs[R : R + 4]
            outs = refs[R + 4 : 2 * R + 4]
            query_ref, held = refs[2 * R + 4 :]
            f, z, _ = here()

            def total(rows):
                return sum(ref[rows, :].astype(f32) for ref in part_refs)

            query_ref[...] = normed(total(slice(0, R * T)), query_gain_ref[...] * fold).astype(bf16)
            key_new = normed(total(slice(R * T, (R + 1) * T)), key_gain_ref[...]).astype(bf16)
            value_new = total(slice((R + 1) * T, (R + 2) * T)).astype(bf16)
            value_new = jnp.concatenate([value_new, jnp.ones((T, H), bf16)], axis=1)
            step = min(512, cached)
            eye = lax.broadcasted_iota(jnp.int32, (T, H), 0) == lax.broadcasted_iota(
                jnp.int32, (T, H), 1
            )

            def block(d, carry):
                query = query_ref[pl.ds(pl.multiple_of(d * T, T), T), :]
                weights = jnp.exp2(dot_last(query, key_new)).astype(bf16)
                sums = dot(weights, value_new)
                for j in range(0, cached, step):
                    weights = jnp.exp2(dot(query, keys_ref[:, j : j + step])).astype(bf16)
                    sums = sums + dot(weights, values_ref[j : j + step, :])
                held[d, :T] = sums[:, :H].astype(bf16)
                row = jnp.sum(jnp.where(eye, sums[:, H:], 0.0), axis=0, keepdims=True)
                high = row.astype(bf16).astype(f32)
                low = row - high
                which = lax.broadcasted_iota(jnp.int32, (tail, H), 0)
                held[d, T:] = jnp.where(which == 0, high, jnp.where(which == 1, low, 0.0)).astype(bf16)
                return carry

            lax.fori_loop(0, R, block, 0, unroll=min(R, 4))
            for s in range(R):
                outs[s][...] = held[f ^ z ^ s]

        sums = call(
            attend,
            "attend",
            (*parts, keys_t, values_one, query_gain, key_gain),
            [jax.ShapeDtypeStruct((T + tail, H), bf16)] * R,
            [pltpu.VMEM((R * T, H), bf16), pltpu.VMEM((R, T + tail, H), bf16)],
            flops=4 * R * T * (cached + T) * H,
        )
        sums = [sums[0]] + [over_row(sums[s], s) for s in range(1, R)]

        def gradient(*refs):
            cot_ref, gate_ref = refs[:2]
            rows_refs = refs[2 : 2 + R]
            own_ref, away_ref = refs[2 + R :]
            f, z, q = here()
            scaled = (cot_ref[...].astype(f32) * gate_ref[...]).astype(bf16)
            for s in range(R):
                part = dot_last(scaled, rows_refs[s][...]).astype(bf16)
                even, odd = part[:, :H], part[:, H:]
                m = f ^ s ^ z
                own_ref[m] = jnp.where(q == 0, even, odd)
                away_ref[m] = jnp.where(q == 0, odd, even)

        slots = jax.ShapeDtypeStruct((R, T, H), bf16)
        grad_own, grad_away = call(
            gradient,
            "gradient",
            (cotangent, out_gate, *out_rows),
            [slots, slots],
            flops=2 * T * R * k * H * wide_out,
        )
        grad_away = across_chip(grad_away)

        def finish(*refs):
            sum_refs = refs[:R]
            own_ref, away_ref = refs[R : R + 2]
            outs = refs[R + 2 :]
            numerators = sum(ref[:T, :].astype(f32) for ref in sum_refs)
            row = sum(ref[T : T + 1, :].astype(f32) + ref[T + 1 : T + 2, :].astype(f32) for ref in sum_refs)
            eye = lax.broadcasted_iota(jnp.int32, (T, H), 0) == lax.broadcasted_iota(
                jnp.int32, (T, H), 1
            )
            totals = jnp.sum(jnp.where(eye, row, 0.0), axis=1, keepdims=True)
            attention = (numerators / totals).astype(bf16)
            for m in range(R):
                outs[m][:T] = attention
                outs[m][T:] = (own_ref[m].astype(f32) + away_ref[m].astype(f32)).astype(bf16)

        pairs = call(
            finish,
            "finish",
            (*sums, grad_own, grad_away),
            [jax.ShapeDtypeStruct((2 * T, H), bf16)] * R,
        )
        pairs = [pairs[0]] + [over_z(pairs[m], m) for m in range(1, R)]
        pairs_other = [across_chip(x) for x in pairs]

        def output(*refs):
            mine_refs, other_refs, rows_refs = refs[:R], refs[R : 2 * R], refs[2 * R : 3 * R]
            tokens_ref, gate_ref, layer_ref, grad_ref, held = refs[3 * R :]
            f, z, q = here()
            grad = jnp.zeros((T, H), f32)
            for m in range(R):
                own, away = mine_refs[m][:T], other_refs[m][:T]
                held[z ^ m, :, :H] = jnp.where(q == 0, own, away)
                held[z ^ m, :, H:] = jnp.where(q == 0, away, own)
                grad = grad + mine_refs[m][T:].astype(f32)
            grad_ref[...] = grad.astype(bf16)
            branch = sum(dot(held[f ^ s], rows_refs[s][...]) for s in range(R))
            layer_ref[...] = (tokens_ref[...].astype(f32) + gate_ref[...] * branch).astype(bf16)

        layer_out, attention_cotangent = call(
            output,
            "output",
            (*pairs, *pairs_other, *out_rows, tokens, out_gate),
            [jax.ShapeDtypeStruct((T, wide_out), bf16), jax.ShapeDtypeStruct((T, H), bf16)],
            [pltpu.VMEM((R, T, k * H), bf16)],
            flops=2 * T * R * k * H * wide_out,
        )
        return layer_out, attention_cotangent

    spread = P("row", "col")
    return jax.shard_map(
        body,
        mesh=mesh,
        in_specs=(spread,) * 7 + (P(), P(), P("col"), spread),
        out_specs=(spread, spread),
        check_vma=False,
    )
```

```python
import math

import jax
import jax.numpy as jnp
from jax import lax
from jax.experimental import pallas as pl
from jax.experimental.pallas import tpu as pltpu
from jax.sharding import PartitionSpec as P

epsilon = 1e-06
both = ("row", "col")
f32 = jnp.float32
bf16 = jnp.bfloat16
tail = 16


def size_of(arrays):
    return sum(math.prod(a.shape) * jnp.dtype(a.dtype).itemsize for a in arrays)


def call(kernel, name, operands, outs, scratch=(), far=0):
    moved = size_of(operands) + size_of(outs)
    held = moved + size_of(scratch)
    whole = pl.BlockSpec(memory_space=pltpu.VMEM)
    fetched = [pltpu.VMEM(a.shape, a.dtype) for a in operands[:far]]

    def fetch(*refs):
        n = len(operands) + len(outs)
        landed, sems = refs[n : n + far], refs[-1]
        copies = [pltpu.make_async_copy(refs[i], landed[i], sems.at[i]) for i in range(far)]
        for copy in copies:
            copy.start()
        for copy in copies:
            copy.wait()
        kernel(*landed, *refs[far:n], *refs[n + far : -1])

    return pl.pallas_call(
        fetch if far else kernel,
        out_shape=list(outs),
        in_specs=[pl.BlockSpec(memory_space=pl.ANY)] * far + [whole] * (len(operands) - far),
        out_specs=[whole] * len(outs),
        scratch_shapes=[*fetched, *scratch] + ([pltpu.SemaphoreType.DMA((far,))] if far else []),
        compiler_params=pltpu.CompilerParams(vmem_limit_bytes=2 * held + (12 << 20)),
        cost_estimate=pl.CostEstimate(flops=0, bytes_accessed=0, transcendentals=0),
        name=name,
    )(*(pltpu.with_memory_space_constraint(a, pltpu.HBM) for a in operands[:far]), *operands[far:])


def dot(a, b):
    return jnp.dot(a, b, preferred_element_type=f32)


def dot_last(a, b):
    return lax.dot_general(a, b, (((1,), (1,)), ((), ())), preferred_element_type=f32)


def normed(wide, gain):
    mean_square = jnp.mean(wide * wide, axis=-1, keepdims=True)
    return wide * lax.rsqrt(mean_square + epsilon) * gain


def solution(mesh):
    R, C = mesh.shape["row"], mesh.shape["col"]
    k = C // R
    assert C == R * k and k == 2 and R & (R - 1) == 0

    def here():
        f, c = lax.axis_index("row"), lax.axis_index("col")
        return f, c // k, c % k

    def route(to):
        return [
            (r * C + z * k + q, (lambda a, b, e: a * C + b * k + e)(*to(r, z, q)))
            for r in range(R)
            for z in range(R)
            for q in range(k)
        ]

    def across_chip(x):
        return lax.ppermute(x, both, route(lambda r, z, q: (r, z, q ^ 1)))

    def over_row(x, s):
        return lax.ppermute(x, both, route(lambda r, z, q: (r ^ s, z, q)))

    def over_z(x, m):
        return lax.ppermute(x, both, route(lambda r, z, q: (r, z ^ m, q)))

    def turned(x, d):
        return lax.ppermute(x, both, route(lambda r, z, q: (z, r ^ z ^ d, q)))

    def body(
        tokens,
        w_query,
        w_key,
        w_value,
        w_out,
        key_cache,
        value_cache,
        query_gain,
        key_gain,
        out_gate,
        cotangent,
    ):
        T, F = tokens.shape
        H = query_gain.shape[0]
        cached = key_cache.shape[0]
        wide_out = w_out.shape[1]
        assert w_query.shape == (k * F, H) and w_out.shape == (k * H, wide_out) and T == H
        query_gain = query_gain.reshape(1, H)
        key_gain = key_gain.reshape(1, H)
        out_gate = out_gate.reshape(1, wide_out)
        fold = H ** (-0.5) * math.log2(math.e)

        near = [s for s in range(1, R) if s & (s - 1) == 0]
        out_rows = {0: w_out, **{s: over_row(w_out, s) for s in near}}
        order = [d for d in range(R) if d.bit_count() % 2 == 0][::-1]
        mine = {d: turned(tokens, d) for d in order}
        mine.update({d ^ 1: over_z(mine[d], 1) for d in order})
        half = k * H // 2
        for s in range(1, R):
            low = s & -s
            top = s ^ low
            if top in near:
                out_rows[s] = (
                    over_row(out_rows[top][:half], low),
                    over_row(out_rows[low][half:], top),
                )
            elif top:
                out_rows[s] = (over_row(w_out, s),)

        def prepare(key_ref, value_ref, wq, wk, wv, qg, kg, key_out, value_out, weight_out, gain_out):
            key = normed(key_ref[...].astype(f32), kg[...])
            key_out[...] = key.T.astype(bf16)
            value_out[:, :H] = value_ref[...]
            value_out[:, H:] = jnp.ones((cached, H), bf16)
            weight_out[:, :H] = wq[...]
            weight_out[:, H : 2 * H] = wk[...]
            weight_out[:, 2 * H :] = wv[...]
            gain_out[0:1, :] = qg[...] * fold
            gain_out[1:2, :] = kg[...]

        keys_t, values_one, weights, gains = call(
            prepare,
            "prepare",
            (key_cache, value_cache, w_query, w_key, w_value, query_gain, key_gain),
            [
                jax.ShapeDtypeStruct((H, cached), bf16),
                jax.ShapeDtypeStruct((cached, 2 * H), bf16),
                jax.ShapeDtypeStruct((k * F, 3 * H), bf16),
                jax.ShapeDtypeStruct((2, H), f32),
            ],
            far=7,
        )

        def project(*refs):
            mine_refs, other_refs, weight_ref = refs[:R], refs[R : 2 * R], refs[2 * R]
            outs, held = refs[2 * R + 1 : 3 * R + 1], refs[-1]
            f, z, q = here()
            w_mine = weight_ref[pl.ds(pl.multiple_of(q * F, F), F), :]
            w_other = weight_ref[pl.ds(pl.multiple_of((1 - q) * F, F), F), :]
            for d in range(R):
                part = (dot(mine_refs[d][...], w_mine) + dot(other_refs[d][...], w_other)).astype(bf16)
                block = f ^ z ^ d
                rows = pl.ds(pl.multiple_of(block * T, T), T)
                for s in range(R):
                    outs[s][rows, :] = part[:, :H]
                held[block, :T] = part[:, H : 2 * H]
                held[block, T:] = part[:, 2 * H :]
            for s in range(R):
                outs[s][R * T :, :] = held[f ^ s]

        joined = lax.optimization_barrier(
            (
                list(mine.values()),
                [out_rows[s] for s in range(1, R)],
                [keys_t, values_one, weights, gains],
            )
        )
        slots, out_rows = dict(zip(mine, joined[0])), [w_out, *joined[1]]
        slots = [slots[d] for d in range(R)]
        keys_t, values_one, weights, gains = joined[2]
        out_rows = [x if not isinstance(x, tuple) else x[0] if len(x) == 1 else jnp.concatenate(x) for x in out_rows]
        slots_other = [across_chip(x) for x in slots]
        parts = call(
            project,
            "project",
            (*slots, *slots_other, weights),
            [jax.ShapeDtypeStruct(((R + 2) * T, H), bf16)] * R,
            [pltpu.VMEM((R, 2 * T, H), bf16)],
        )
        parts = [parts[0]] + [over_row(parts[s], s) for s in range(1, R)]
        def gradient(*refs):
            cot_ref, gate_ref = refs[:2]
            rows_refs, outs, held = refs[2 : 2 + R], refs[2 + R : 2 + 2 * R], refs[-1]
            f, z, q = here()
            scaled = (cot_ref[...].astype(f32) * gate_ref[...]).astype(bf16)
            for s in range(R):
                part = dot_last(scaled, rows_refs[s][...]).astype(bf16)
                even, odd = part[:, :H], part[:, H:]
                held[f ^ s, :T] = jnp.where(q == 0, even, odd)
                held[f ^ s, T:] = jnp.where(q == 0, odd, even)
            for m in range(R):
                outs[m][...] = held[z ^ m]

        sent = jax.ShapeDtypeStruct((k * T, H), bf16)
        grads = call(
            gradient,
            "gradient",
            (cotangent, out_gate, *out_rows),
            [sent] * R,
            [pltpu.VMEM((R, k * T, H), bf16)],
        )
        grads = [grads[0]] + [over_z(grads[m], m) for m in range(1, R)]

        parts, grads = lax.optimization_barrier((parts, grads))

        def join(*refs):
            own_ref, away_ref = refs[R:]
            both_heads = sum(ref[...].astype(f32) for ref in refs[:R])
            own_ref[...] = both_heads[:T].astype(bf16)
            away_ref[...] = both_heads[T:].astype(bf16)

        grad_own, grad_away = call(join, "join", grads, [jax.ShapeDtypeStruct((T, H), bf16)] * 2)
        grad_away = across_chip(grad_away)

        def attend(*refs):
            part_refs = refs[:R]
            keys_ref, values_ref, gain_ref = refs[R : R + 3]
            outs = refs[R + 3 : 2 * R + 3]
            query_ref, held = refs[2 * R + 3 :]
            f, _, _ = here()

            def total(rows):
                return sum(ref[rows, :].astype(f32) for ref in part_refs)

            query_ref[...] = normed(total(slice(0, R * T)), gain_ref[0:1, :]).astype(bf16)
            key_new = normed(total(slice(R * T, (R + 1) * T)), gain_ref[1:2, :]).astype(bf16)
            value_new = total(slice((R + 1) * T, (R + 2) * T)).astype(bf16)
            value_new = jnp.concatenate([value_new, jnp.ones_like(value_new)], axis=1)
            step = min(512, cached)
            eye = lax.broadcasted_iota(jnp.int32, (T, H), 0) == lax.broadcasted_iota(
                jnp.int32, (T, H), 1
            )

            def block(d, carry):
                query = query_ref[pl.ds(pl.multiple_of(d * T, T), T), :]
                weights = jnp.exp2(dot_last(query, key_new)).astype(bf16)
                sums = dot(weights, value_new)
                for j in range(0, cached, step):
                    weights = jnp.exp2(dot(query, keys_ref[:, j : j + step])).astype(bf16)
                    sums = sums + dot(weights, values_ref[j : j + step, :])
                held[d, :T] = sums[:, :H].astype(bf16)
                row = jnp.sum(jnp.where(eye, sums[:, H:], 0.0), axis=0, keepdims=True)
                high = row.astype(bf16).astype(f32)
                low = row - high
                which = lax.broadcasted_iota(jnp.int32, (tail, H), 0)
                held[d, T:] = jnp.where(which == 0, high, jnp.where(which == 1, low, 0.0)).astype(bf16)
                return carry

            lax.fori_loop(0, R, block, 0, unroll=min(R, 4))
            for s in range(R):
                outs[s][...] = held[f ^ s]

        sums = call(
            attend,
            "attend",
            (*parts, keys_t, values_one, gains),
            [jax.ShapeDtypeStruct((T + tail, H), bf16)] * R,
            [pltpu.VMEM((R * T, H), bf16), pltpu.VMEM((R, T + tail, H), bf16)],
        )
        sums = [sums[0]] + [over_row(sums[s], s) for s in range(1, R)]

        def finish(*refs):
            sum_refs, out = refs[:R], refs[R]
            numerators = sum(ref[:T, :].astype(f32) for ref in sum_refs)
            row = sum(ref[T : T + 1, :].astype(f32) + ref[T + 1 : T + 2, :].astype(f32) for ref in sum_refs)
            eye = lax.broadcasted_iota(jnp.int32, (T, H), 0) == lax.broadcasted_iota(
                jnp.int32, (T, H), 1
            )
            totals = jnp.sum(jnp.where(eye, row, 0.0), axis=1, keepdims=True)
            out[...] = (numerators / totals).astype(bf16)

        (attention,) = call(finish, "finish", sums, [jax.ShapeDtypeStruct((T, H), bf16)])
        heads = {0: attention}
        for bit in near:
            heads.update({m | bit: over_z(heads[m], bit) for m in list(heads)})
        heads = [heads[m] for m in range(R)]
        heads = [heads[0], *lax.optimization_barrier(heads[1:])]
        heads_other = [across_chip(x) for x in heads]

        def output(*refs):
            tokens_ref, gate_ref, own_ref, away_ref = refs[:4]
            mine_refs, other_refs, rows_refs = (refs[i * R + 4 : (i + 1) * R + 4] for i in range(3))
            layer_ref, grad_ref, held = refs[3 * R + 4 :]
            f, z, q = here()
            grad_ref[...] = (own_ref[...].astype(f32) + away_ref[...].astype(f32)).astype(bf16)
            for m in range(R):
                own, away = mine_refs[m][...], other_refs[m][...]
                held[z ^ m, :, :H] = jnp.where(q == 0, own, away)
                held[z ^ m, :, H:] = jnp.where(q == 0, away, own)
            branch = sum(dot(held[f ^ s], rows_refs[s][...]) for s in range(R))
            layer_ref[...] = (tokens_ref[...].astype(f32) + gate_ref[...] * branch).astype(bf16)

        layer_out, attention_cotangent = call(
            output,
            "output",
            (tokens, out_gate, grad_own, grad_away, *heads, *heads_other, *out_rows),
            [jax.ShapeDtypeStruct((T, wide_out), bf16), jax.ShapeDtypeStruct((T, H), bf16)],
            [pltpu.VMEM((R, T, k * H), bf16)],
        )
        return layer_out, attention_cotangent

    spread = P("row", "col")
    return jax.shard_map(
        body,
        mesh=mesh,
        in_specs=(spread,) * 7 + (P(), P(), P("col"), spread),
        out_specs=(spread, spread),
        check_vma=False,
    )
```

```python
import math

import jax
import jax.numpy as jnp
from jax import lax
from jax.experimental import pallas as pl
from jax.experimental.pallas import tpu as pltpu
from jax.sharding import PartitionSpec as P

epsilon = 1e-06
both = ("row", "col")
f32 = jnp.float32
bf16 = jnp.bfloat16
tail = 16


def size_of(arrays):
    return sum(math.prod(a.shape) * jnp.dtype(a.dtype).itemsize for a in arrays)


def call(kernel, name, operands, outs, scratch=(), far=0):
    moved = size_of(operands) + size_of(outs)
    held = moved + size_of(scratch)
    whole = pl.BlockSpec(memory_space=pltpu.VMEM)
    fetched = [pltpu.VMEM(a.shape, a.dtype) for a in operands[:far]]

    def fetch(*refs):
        n = len(operands) + len(outs)
        landed, sems = refs[n : n + far], refs[-1]
        copies = [pltpu.make_async_copy(refs[i], landed[i], sems.at[i]) for i in range(far)]
        for copy in copies:
            copy.start()
        for copy in copies:
            copy.wait()
        kernel(*landed, *refs[far:n], *refs[n + far : -1])

    return pl.pallas_call(
        fetch if far else kernel,
        out_shape=list(outs),
        in_specs=[pl.BlockSpec(memory_space=pl.ANY)] * far + [whole] * (len(operands) - far),
        out_specs=[whole] * len(outs),
        scratch_shapes=[*fetched, *scratch] + ([pltpu.SemaphoreType.DMA((far,))] if far else []),
        compiler_params=pltpu.CompilerParams(vmem_limit_bytes=2 * held + (12 << 20)),
        cost_estimate=pl.CostEstimate(flops=0, bytes_accessed=0, transcendentals=0),
        name=name,
    )(*(pltpu.with_memory_space_constraint(a, pltpu.HBM) for a in operands[:far]), *operands[far:])


def dot(a, b):
    return jnp.dot(a, b, preferred_element_type=f32)


def dot_last(a, b):
    return lax.dot_general(a, b, (((1,), (1,)), ((), ())), preferred_element_type=f32)


def normed(wide, gain):
    mean_square = jnp.mean(wide * wide, axis=-1, keepdims=True)
    return wide * lax.rsqrt(mean_square + epsilon) * gain


def solution(mesh):
    R, C = mesh.shape["row"], mesh.shape["col"]
    k = C // R
    assert C == R * k and k == 2 and R & (R - 1) == 0

    def here():
        f, c = lax.axis_index("row"), lax.axis_index("col")
        return f, c // k, c % k

    def route(to):
        return [
            (r * C + z * k + q, (lambda a, b, e: a * C + b * k + e)(*to(r, z, q)))
            for r in range(R)
            for z in range(R)
            for q in range(k)
        ]

    def across_chip(x):
        return lax.ppermute(x, both, route(lambda r, z, q: (r, z, q ^ 1)))

    def over_row(x, s):
        return lax.ppermute(x, both, route(lambda r, z, q: (r ^ s, z, q)))

    def over_z(x, m):
        return lax.ppermute(x, both, route(lambda r, z, q: (r, z ^ m, q)))

    def turned(x, d):
        return lax.ppermute(x, both, route(lambda r, z, q: (z, r ^ z ^ d, q)))

    def body(
        tokens,
        w_query,
        w_key,
        w_value,
        w_out,
        key_cache,
        value_cache,
        query_gain,
        key_gain,
        out_gate,
        cotangent,
    ):
        T, F = tokens.shape
        H = query_gain.shape[0]
        cached = key_cache.shape[0]
        wide_out = w_out.shape[1]
        assert w_query.shape == (k * F, H) and w_out.shape == (k * H, wide_out) and T == H
        query_gain = query_gain.reshape(1, H)
        key_gain = key_gain.reshape(1, H)
        out_gate = out_gate.reshape(1, wide_out)
        fold = H ** (-0.5) * math.log2(math.e)

        near = [s for s in range(1, R) if s & (s - 1) == 0]
        out_rows = {0: w_out, **{s: over_row(w_out, s) for s in near}}
        order = [d for d in range(R) if d.bit_count() % 2 == 0][::-1]
        mine = {d: turned(tokens, d) for d in order}
        mine.update({d ^ 1: over_z(mine[d], 1) for d in order})
        half = k * H // 2
        for s in range(1, R):
            low = s & -s
            top = s ^ low
            if top in near:
                out_rows[s] = (
                    over_row(out_rows[top][:half], low),
                    over_row(out_rows[low][half:], top),
                )
            elif top:
                out_rows[s] = (over_row(w_out, s),)

        def prepare(key_ref, value_ref, wq, wk, wv, qg, kg, key_out, value_out, weight_out, gain_out):
            key = normed(key_ref[...].astype(f32), kg[...])
            key_out[...] = key.T.astype(bf16)
            value_out[:, :H] = value_ref[...]
            value_out[:, H:] = jnp.ones((cached, H), bf16)
            weight_out[:, :H] = wq[...]
            weight_out[:, H : 2 * H] = wk[...]
            weight_out[:, 2 * H :] = wv[...]
            gain_out[0:1, :] = qg[...] * fold
            gain_out[1:2, :] = kg[...]

        keys_t, values_one, weights, gains = call(
            prepare,
            "prepare",
            (key_cache, value_cache, w_query, w_key, w_value, query_gain, key_gain),
            [
                jax.ShapeDtypeStruct((H, cached), bf16),
                jax.ShapeDtypeStruct((cached, 2 * H), bf16),
                jax.ShapeDtypeStruct((k * F, 3 * H), bf16),
                jax.ShapeDtypeStruct((2, H), f32),
            ],
            far=7,
        )

        def project(*refs):
            mine_refs, other_refs, weight_ref = refs[:R], refs[R : 2 * R], refs[2 * R]
            outs, held = refs[2 * R + 1 : 3 * R + 1], refs[-1]
            f, z, q = here()
            w_mine = weight_ref[pl.ds(pl.multiple_of(q * F, F), F), :]
            w_other = weight_ref[pl.ds(pl.multiple_of((1 - q) * F, F), F), :]
            whole_mine = jnp.concatenate([ref[...] for ref in mine_refs])
            whole_other = jnp.concatenate([ref[...] for ref in other_refs])
            whole = (dot(whole_mine, w_mine) + dot(whole_other, w_other)).astype(bf16)
            for d in range(R):
                part = whole[d * T : (d + 1) * T]
                block = f ^ z ^ d
                rows = pl.ds(pl.multiple_of(block * T, T), T)
                for s in range(R):
                    outs[s][rows, :] = part[:, :H]
                held[block, :T] = part[:, H : 2 * H]
                held[block, T:] = part[:, 2 * H :]
            for s in range(R):
                outs[s][R * T :, :] = held[f ^ s]

        joined = lax.optimization_barrier(
            (
                list(mine.values()),
                [out_rows[s] for s in range(1, R)],
                [keys_t, values_one, weights, gains],
            )
        )
        slots, out_rows = dict(zip(mine, joined[0])), [w_out, *joined[1]]
        slots = [slots[d] for d in range(R)]
        keys_t, values_one, weights, gains = joined[2]
        out_rows = [x if not isinstance(x, tuple) else x[0] if len(x) == 1 else jnp.concatenate(x) for x in out_rows]
        slots_other = [across_chip(x) for x in slots]
        parts = call(
            project,
            "project",
            (*slots, *slots_other, weights),
            [jax.ShapeDtypeStruct(((R + 2) * T, H), bf16)] * R,
            [pltpu.VMEM((R, 2 * T, H), bf16)],
        )
        parts = [parts[0]] + [over_row(parts[s], s) for s in range(1, R)]
        def gradient(*refs):
            cot_ref, gate_ref = refs[:2]
            rows_refs, outs, held = refs[2 : 2 + R], refs[2 + R : 2 + 2 * R], refs[-1]
            f, z, q = here()
            scaled = (cot_ref[...].astype(f32) * gate_ref[...]).astype(bf16)
            for s in range(R):
                part = dot_last(scaled, rows_refs[s][...]).astype(bf16)
                even, odd = part[:, :H], part[:, H:]
                held[f ^ s, :T] = jnp.where(q == 0, even, odd)
                held[f ^ s, T:] = jnp.where(q == 0, odd, even)
            for m in range(R):
                outs[m][...] = held[z ^ m]

        sent = jax.ShapeDtypeStruct((k * T, H), bf16)
        grads = call(
            gradient,
            "gradient",
            (cotangent, out_gate, *out_rows),
            [sent] * R,
            [pltpu.VMEM((R, k * T, H), bf16)],
        )
        grads = [grads[0]] + [over_z(grads[m], m) for m in range(1, R)]

        def attend(*refs):
            part_refs = refs[:R]
            keys_ref, values_ref, gain_ref = refs[R : R + 3]
            outs = refs[R + 3 : 2 * R + 3]
            query_ref, held = refs[2 * R + 3 :]
            f, _, _ = here()

            def total(rows):
                return sum(ref[rows, :].astype(f32) for ref in part_refs)

            query_ref[...] = normed(total(slice(0, R * T)), gain_ref[0:1, :]).astype(bf16)
            key_new = normed(total(slice(R * T, (R + 1) * T)), gain_ref[1:2, :]).astype(bf16)
            value_new = total(slice((R + 1) * T, (R + 2) * T)).astype(bf16)
            value_new = jnp.concatenate([value_new, jnp.ones_like(value_new)], axis=1)
            step = min(512, cached)
            eye = lax.broadcasted_iota(jnp.int32, (T, H), 0) == lax.broadcasted_iota(
                jnp.int32, (T, H), 1
            )

            def block(d, carry):
                query = query_ref[pl.ds(pl.multiple_of(d * T, T), T), :]
                weights = jnp.exp2(dot_last(query, key_new)).astype(bf16)
                sums = dot(weights, value_new)
                for j in range(0, cached, step):
                    weights = jnp.exp2(dot(query, keys_ref[:, j : j + step])).astype(bf16)
                    sums = sums + dot(weights, values_ref[j : j + step, :])
                held[d, :T] = sums[:, :H].astype(bf16)
                row = jnp.sum(jnp.where(eye, sums[:, H:], 0.0), axis=0, keepdims=True)
                high = row.astype(bf16).astype(f32)
                low = row - high
                which = lax.broadcasted_iota(jnp.int32, (tail, H), 0)
                held[d, T:] = jnp.where(which == 0, high, jnp.where(which == 1, low, 0.0)).astype(bf16)
                return carry

            lax.fori_loop(0, R, block, 0, unroll=min(R, 4))
            for s in range(R):
                outs[s][...] = held[f ^ s]

        sums = call(
            attend,
            "attend",
            (*parts, keys_t, values_one, gains),
            [jax.ShapeDtypeStruct((T + tail, H), bf16)] * R,
            [pltpu.VMEM((R * T, H), bf16), pltpu.VMEM((R, T + tail, H), bf16)],
        )
        sums = [sums[0]] + [over_row(sums[s], s) for s in range(1, R)]

        sums, grads = lax.optimization_barrier((sums, grads))

        def join(*refs):
            own_ref, away_ref = refs[R:]
            both_heads = sum(ref[...].astype(f32) for ref in refs[:R])
            own_ref[...] = both_heads[:T].astype(bf16)
            away_ref[...] = both_heads[T:].astype(bf16)

        grad_own, grad_away = call(join, "join", grads, [jax.ShapeDtypeStruct((T, H), bf16)] * 2)
        grad_away = across_chip(grad_away)

        def finish(*refs):
            sum_refs, out = refs[:R], refs[R]
            numerators = sum(ref[:T, :].astype(f32) for ref in sum_refs)
            row = sum(ref[T : T + 1, :].astype(f32) + ref[T + 1 : T + 2, :].astype(f32) for ref in sum_refs)
            eye = lax.broadcasted_iota(jnp.int32, (T, H), 0) == lax.broadcasted_iota(
                jnp.int32, (T, H), 1
            )
            totals = jnp.sum(jnp.where(eye, row, 0.0), axis=1, keepdims=True)
            out[...] = (numerators / totals).astype(bf16)

        (attention,) = call(finish, "finish", sums, [jax.ShapeDtypeStruct((T, H), bf16)])
        heads = [attention] + [over_z(attention, m) for m in range(1, R)]
        heads_other = [across_chip(x) for x in heads]

        def output(*refs):
            tokens_ref, gate_ref, own_ref, away_ref = refs[:4]
            mine_refs, other_refs, rows_refs = (refs[i * R + 4 : (i + 1) * R + 4] for i in range(3))
            layer_ref, grad_ref, held = refs[3 * R + 4 :]
            f, z, q = here()
            grad_ref[...] = (own_ref[...].astype(f32) + away_ref[...].astype(f32)).astype(bf16)
            for m in range(R):
                own, away = mine_refs[m][...], other_refs[m][...]
                held[z ^ m, :, :H] = jnp.where(q == 0, own, away)
                held[z ^ m, :, H:] = jnp.where(q == 0, away, own)
            branch = sum(dot(held[f ^ s], rows_refs[s][...]) for s in range(R))
            layer_ref[...] = (tokens_ref[...].astype(f32) + gate_ref[...] * branch).astype(bf16)

        layer_out, attention_cotangent = call(
            output,
            "output",
            (tokens, out_gate, grad_own, grad_away, *heads, *heads_other, *out_rows),
            [jax.ShapeDtypeStruct((T, wide_out), bf16), jax.ShapeDtypeStruct((T, H), bf16)],
            [pltpu.VMEM((R, T, k * H), bf16)],
        )
        return layer_out, attention_cotangent

    spread = P("row", "col")
    return jax.shard_map(
        body,
        mesh=mesh,
        in_specs=(spread,) * 7 + (P(), P(), P("col"), spread),
        out_specs=(spread, spread),
        check_vma=False,
    )
```

```python
import math

import jax
import jax.numpy as jnp
from jax import lax
from jax.experimental import pallas as pl
from jax.experimental.pallas import tpu as pltpu
from jax.sharding import PartitionSpec as P

epsilon = 1e-06
both = ("row", "col")
f32 = jnp.float32
bf16 = jnp.bfloat16
tail = 16


def size_of(arrays):
    return sum(math.prod(a.shape) * jnp.dtype(a.dtype).itemsize for a in arrays)


def call(kernel, name, operands, outs, scratch=(), far=0):
    moved = size_of(operands) + size_of(outs)
    held = moved + size_of(scratch)
    whole = pl.BlockSpec(memory_space=pltpu.VMEM)
    fetched = [pltpu.VMEM(a.shape, a.dtype) for a in operands[:far]]

    def fetch(*refs):
        n = len(operands) + len(outs)
        landed, sems = refs[n : n + far], refs[-1]
        copies = [pltpu.make_async_copy(refs[i], landed[i], sems.at[i]) for i in range(far)]
        for copy in copies:
            copy.start()
        for copy in copies:
            copy.wait()
        kernel(*landed, *refs[far:n], *refs[n + far : -1])

    return pl.pallas_call(
        fetch if far else kernel,
        out_shape=list(outs),
        in_specs=[pl.BlockSpec(memory_space=pl.ANY)] * far + [whole] * (len(operands) - far),
        out_specs=[whole] * len(outs),
        scratch_shapes=[*fetched, *scratch] + ([pltpu.SemaphoreType.DMA((far,))] if far else []),
        compiler_params=pltpu.CompilerParams(vmem_limit_bytes=2 * held + (12 << 20)),
        cost_estimate=pl.CostEstimate(flops=0, bytes_accessed=0, transcendentals=0),
        name=name,
    )(*(pltpu.with_memory_space_constraint(a, pltpu.HBM) for a in operands[:far]), *operands[far:])


def dot(a, b):
    return jnp.dot(a, b, preferred_element_type=f32)


def dot_last(a, b):
    return lax.dot_general(a, b, (((1,), (1,)), ((), ())), preferred_element_type=f32)


def normed(wide, gain):
    mean_square = jnp.mean(wide * wide, axis=-1, keepdims=True)
    return wide * lax.rsqrt(mean_square + epsilon) * gain


def solution(mesh):
    R, C = mesh.shape["row"], mesh.shape["col"]
    k = C // R
    assert C == R * k and k == 2 and R & (R - 1) == 0

    def here():
        f, c = lax.axis_index("row"), lax.axis_index("col")
        return f, c // k, c % k

    def route(to):
        return [
            (r * C + z * k + q, (lambda a, b, e: a * C + b * k + e)(*to(r, z, q)))
            for r in range(R)
            for z in range(R)
            for q in range(k)
        ]

    def across_chip(x):
        return lax.ppermute(x, both, route(lambda r, z, q: (r, z, q ^ 1)))

    def over_row(x, s):
        return lax.ppermute(x, both, route(lambda r, z, q: (r ^ s, z, q)))

    def over_z(x, m):
        return lax.ppermute(x, both, route(lambda r, z, q: (r, z ^ m, q)))

    def turned(x, d):
        return lax.ppermute(x, both, route(lambda r, z, q: (z, r ^ z ^ d, q ^ (r == z == d))))

    def body(
        tokens,
        w_query,
        w_key,
        w_value,
        w_out,
        key_cache,
        value_cache,
        query_gain,
        key_gain,
        out_gate,
        cotangent,
    ):
        T, F = tokens.shape
        H = query_gain.shape[0]
        cached = key_cache.shape[0]
        wide_out = w_out.shape[1]
        assert w_query.shape == (k * F, H) and w_out.shape == (k * H, wide_out) and T == H
        query_gain = query_gain.reshape(1, H)
        key_gain = key_gain.reshape(1, H)
        out_gate = out_gate.reshape(1, wide_out)
        fold = H ** (-0.5) * math.log2(math.e)

        near = [s for s in range(1, R) if s & (s - 1) == 0]
        out_rows = {0: w_out, **{s: over_row(w_out, s) for s in near}}
        order = [d for d in range(R) if d.bit_count() % 2 == 0][::-1]
        mine = {d: turned(tokens, d) for d in order}
        mine.update({d ^ 1: over_z(mine[d], 1) for d in order})
        half = k * H // 2
        for s in range(1, R):
            low = s & -s
            top = s ^ low
            if top in near:
                out_rows[s] = (
                    over_row(out_rows[top][:half], low),
                    over_row(out_rows[low][half:], top),
                )
            elif top:
                out_rows[s] = (over_row(w_out, s),)

        def prepare(key_ref, value_ref, wq, wk, wv, qg, kg, key_out, value_out, weight_out, gain_out):
            key = normed(key_ref[...].astype(f32), kg[...])
            key_out[...] = key.T.astype(bf16)
            value_out[:, :H] = value_ref[...]
            value_out[:, H:] = jnp.ones((cached, H), bf16)
            weight_out[:, :H] = wq[...]
            weight_out[:, H : 2 * H] = wk[...]
            weight_out[:, 2 * H :] = wv[...]
            gain_out[0:1, :] = qg[...] * fold
            gain_out[1:2, :] = kg[...]

        keys_t, values_one, weights, gains = call(
            prepare,
            "prepare",
            (key_cache, value_cache, w_query, w_key, w_value, query_gain, key_gain),
            [
                jax.ShapeDtypeStruct((H, cached), bf16),
                jax.ShapeDtypeStruct((cached, 2 * H), bf16),
                jax.ShapeDtypeStruct((k * F, 3 * H), bf16),
                jax.ShapeDtypeStruct((2, H), f32),
            ],
            far=7,
        )

        def project(*refs):
            mine_refs, other_refs, weight_ref = refs[:R], refs[R : 2 * R], refs[2 * R]
            outs, held = refs[2 * R + 1 : 3 * R + 1], refs[-1]
            f, z, q = here()
            w_mine = weight_ref[pl.ds(pl.multiple_of(q * F, F), F), :]
            w_other = weight_ref[pl.ds(pl.multiple_of((1 - q) * F, F), F), :]
            mine_blocks, other_blocks = [], []
            for d in range(R):
                direct = d if d in order else d ^ 1
                crossed = jnp.logical_and(f == direct, z == d)
                a, b = mine_refs[d][...], other_refs[d][...]
                mine_blocks.append(jnp.where(crossed, b, a))
                other_blocks.append(jnp.where(crossed, a, b))
            whole_mine, whole_other = jnp.concatenate(mine_blocks), jnp.concatenate(other_blocks)
            whole = (dot(whole_mine, w_mine) + dot(whole_other, w_other)).astype(bf16)
            for d in range(R):
                part = whole[d * T : (d + 1) * T]
                block = f ^ z ^ d
                rows = pl.ds(pl.multiple_of(block * T, T), T)
                for s in range(R):
                    outs[s][rows, :] = part[:, :H]
                held[block, :T] = part[:, H : 2 * H]
                held[block, T:] = part[:, 2 * H :]
            for s in range(R):
                outs[s][R * T :, :] = held[f ^ s]

        joined = lax.optimization_barrier(
            (
                list(mine.values()),
                [out_rows[s] for s in range(1, R)],
                [keys_t, values_one, weights, gains],
            )
        )
        slots, out_rows = dict(zip(mine, joined[0])), [w_out, *joined[1]]
        slots = [slots[d] for d in range(R)]
        keys_t, values_one, weights, gains = joined[2]
        out_rows = [x if not isinstance(x, tuple) else x[0] if len(x) == 1 else jnp.concatenate(x) for x in out_rows]
        slots_other = [across_chip(x) for x in slots]
        parts = call(
            project,
            "project",
            (*slots, *slots_other, weights),
            [jax.ShapeDtypeStruct(((R + 2) * T, H), bf16)] * R,
            [pltpu.VMEM((R, 2 * T, H), bf16)],
        )
        far_first = list(range(R - 1, 0, -1))
        sent_parts = lax.optimization_barrier([over_row(parts[s], s) for s in far_first])
        parts = [parts[0], *sent_parts[::-1]]

        def gradient(*refs):
            cot_ref, gate_ref = refs[:2]
            rows_refs, outs, held = refs[2 : 2 + R], refs[2 + R : 2 + 2 * R], refs[-1]
            f, z, q = here()
            scaled = (cot_ref[...].astype(f32) * gate_ref[...]).astype(bf16)
            for s in range(R):
                part = dot_last(scaled, rows_refs[s][...]).astype(bf16)
                even, odd = part[:, :H], part[:, H:]
                held[f ^ s, :T] = jnp.where(q == 0, even, odd)
                held[f ^ s, T:] = jnp.where(q == 0, odd, even)
            for m in range(R):
                outs[m][...] = held[z ^ m]

        sent = jax.ShapeDtypeStruct((k * T, H), bf16)
        grads = call(
            gradient,
            "gradient",
            (cotangent, out_gate, *out_rows),
            [sent] * R,
            [pltpu.VMEM((R, k * T, H), bf16)],
        )
        grads = [grads[0]] + [over_z(grads[m], m) for m in range(1, R)]

        def attend(*refs):
            part_refs = refs[:R]
            keys_ref, values_ref, gain_ref = refs[R : R + 3]
            outs = refs[R + 3 : 2 * R + 3]
            query_ref, held = refs[2 * R + 3 :]
            f, _, _ = here()

            def total(rows):
                return sum(ref[rows, :].astype(f32) for ref in part_refs)

            query_ref[...] = normed(total(slice(0, R * T)), gain_ref[0:1, :]).astype(bf16)
            key_new = normed(total(slice(R * T, (R + 1) * T)), gain_ref[1:2, :]).astype(bf16)
            value_new = total(slice((R + 1) * T, (R + 2) * T)).astype(bf16)
            value_new = jnp.concatenate([value_new, jnp.ones_like(value_new)], axis=1)
            step = min(512, cached)
            eye = lax.broadcasted_iota(jnp.int32, (T, H), 0) == lax.broadcasted_iota(
                jnp.int32, (T, H), 1
            )

            def block(d, carry):
                query = query_ref[pl.ds(pl.multiple_of(d * T, T), T), :]
                weights = jnp.exp2(dot_last(query, key_new)).astype(bf16)
                sums = dot(weights, value_new)
                for j in range(0, cached, step):
                    weights = jnp.exp2(dot(query, keys_ref[:, j : j + step])).astype(bf16)
                    sums = sums + dot(weights, values_ref[j : j + step, :])
                held[d, :T] = sums[:, :H].astype(bf16)
                row = jnp.sum(jnp.where(eye, sums[:, H:], 0.0), axis=0, keepdims=True)
                high = row.astype(bf16).astype(f32)
                low = row - high
                which = lax.broadcasted_iota(jnp.int32, (tail, H), 0)
                held[d, T:] = jnp.where(which == 0, high, jnp.where(which == 1, low, 0.0)).astype(bf16)
                return carry

            lax.fori_loop(0, R, block, 0, unroll=min(R, 4))
            for s in range(R):
                outs[s][...] = held[f ^ s]

        sums = call(
            attend,
            "attend",
            (*parts, keys_t, values_one, gains),
            [jax.ShapeDtypeStruct((T + tail, H), bf16)] * R,
            [pltpu.VMEM((R * T, H), bf16), pltpu.VMEM((R, T + tail, H), bf16)],
        )
        sums = [sums[0]] + [over_row(sums[s], s) for s in range(1, R)]

        sums, grads = lax.optimization_barrier((sums, grads))

        def join(*refs):
            own_ref, away_ref = refs[R:]
            both_heads = sum(ref[...].astype(f32) for ref in refs[:R])
            own_ref[...] = both_heads[:T].astype(bf16)
            away_ref[...] = both_heads[T:].astype(bf16)

        grad_own, grad_away = call(join, "join", grads, [jax.ShapeDtypeStruct((T, H), bf16)] * 2)
        grad_away = across_chip(grad_away)

        def finish(*refs):
            sum_refs, out = refs[:R], refs[R]
            numerators = sum(ref[:T, :].astype(f32) for ref in sum_refs)
            row = sum(ref[T : T + 1, :].astype(f32) + ref[T + 1 : T + 2, :].astype(f32) for ref in sum_refs)
            eye = lax.broadcasted_iota(jnp.int32, (T, H), 0) == lax.broadcasted_iota(
                jnp.int32, (T, H), 1
            )
            totals = jnp.sum(jnp.where(eye, row, 0.0), axis=1, keepdims=True)
            out[...] = (numerators / totals).astype(bf16)

        (attention,) = call(finish, "finish", sums, [jax.ShapeDtypeStruct((T, H), bf16)])
        heads = [attention] + [over_z(attention, m) for m in range(1, R)]
        heads_other = [across_chip(x) for x in heads]

        def output(*refs):
            tokens_ref, gate_ref, own_ref, away_ref = refs[:4]
            mine_refs, other_refs, rows_refs = (refs[i * R + 4 : (i + 1) * R + 4] for i in range(3))
            layer_ref, grad_ref, held = refs[3 * R + 4 :]
            f, z, q = here()
            grad_ref[...] = (own_ref[...].astype(f32) + away_ref[...].astype(f32)).astype(bf16)
            for m in range(R):
                own, away = mine_refs[m][...], other_refs[m][...]
                held[z ^ m, :, :H] = jnp.where(q == 0, own, away)
                held[z ^ m, :, H:] = jnp.where(q == 0, away, own)
            branch = sum(dot(held[f ^ s], rows_refs[s][...]) for s in range(R))
            layer_ref[...] = (tokens_ref[...].astype(f32) + gate_ref[...] * branch).astype(bf16)

        layer_out, attention_cotangent = call(
            output,
            "output",
            (tokens, out_gate, grad_own, grad_away, *heads, *heads_other, *out_rows),
            [jax.ShapeDtypeStruct((T, wide_out), bf16), jax.ShapeDtypeStruct((T, H), bf16)],
            [pltpu.VMEM((R, T, k * H), bf16)],
        )
        return layer_out, attention_cotangent

    spread = P("row", "col")
    return jax.shard_map(
        body,
        mesh=mesh,
        in_specs=(spread,) * 7 + (P(), P(), P("col"), spread),
        out_specs=(spread, spread),
        check_vma=False,
    )
```

```python
import math

import jax
import jax.numpy as jnp
from jax import lax
from jax.experimental import pallas as pl
from jax.experimental.pallas import tpu as pltpu
from jax.sharding import PartitionSpec as P

epsilon = 1e-06
both = ("row", "col")
f32 = jnp.float32
bf16 = jnp.bfloat16
tail = 16


def size_of(arrays):
    return sum(math.prod(a.shape) * jnp.dtype(a.dtype).itemsize for a in arrays)


def call(kernel, name, operands, outs, scratch=(), far=0):
    moved = size_of(operands) + size_of(outs)
    held = moved + size_of(scratch)
    whole = pl.BlockSpec(memory_space=pltpu.VMEM)
    fetched = [pltpu.VMEM(a.shape, a.dtype) for a in operands[:far]]

    def fetch(*refs):
        n = len(operands) + len(outs)
        landed, sems = refs[n : n + far], refs[-1]
        copies = [pltpu.make_async_copy(refs[i], landed[i], sems.at[i]) for i in range(far)]
        for copy in copies:
            copy.start()
        for copy in copies:
            copy.wait()
        kernel(*landed, *refs[far:n], *refs[n + far : -1])

    return pl.pallas_call(
        fetch if far else kernel,
        out_shape=list(outs),
        in_specs=[pl.BlockSpec(memory_space=pl.ANY)] * far + [whole] * (len(operands) - far),
        out_specs=[whole] * len(outs),
        scratch_shapes=[*fetched, *scratch] + ([pltpu.SemaphoreType.DMA((far,))] if far else []),
        compiler_params=pltpu.CompilerParams(vmem_limit_bytes=2 * held + (12 << 20)),
        cost_estimate=pl.CostEstimate(flops=0, bytes_accessed=0, transcendentals=0),
        name=name,
    )(*(pltpu.with_memory_space_constraint(a, pltpu.HBM) for a in operands[:far]), *operands[far:])


def dot(a, b):
    return jnp.dot(a, b, preferred_element_type=f32)


def dot_last(a, b):
    return lax.dot_general(a, b, (((1,), (1,)), ((), ())), preferred_element_type=f32)


def normed(wide, gain):
    mean_square = jnp.mean(wide * wide, axis=-1, keepdims=True)
    return wide * lax.rsqrt(mean_square + epsilon) * gain


def solution(mesh):
    R, C = mesh.shape["row"], mesh.shape["col"]
    k = C // R
    assert C == R * k and k == 2 and R & (R - 1) == 0

    def here():
        f, c = lax.axis_index("row"), lax.axis_index("col")
        return f, c // k, c % k

    def route(to):
        return [
            (r * C + z * k + q, (lambda a, b, e: a * C + b * k + e)(*to(r, z, q)))
            for r in range(R)
            for z in range(R)
            for q in range(k)
        ]

    def across_chip(x):
        return lax.ppermute(x, both, route(lambda r, z, q: (r, z, q ^ 1)))

    def over_row(x, s):
        return lax.ppermute(x, both, route(lambda r, z, q: (r ^ s, z, q)))

    def over_z(x, m):
        return lax.ppermute(x, both, route(lambda r, z, q: (r, z ^ m, q)))

    def turned(x, d):
        return lax.ppermute(x, both, route(lambda r, z, q: (z, r ^ z ^ d, q ^ (r == z == d))))

    def body(
        tokens,
        w_query,
        w_key,
        w_value,
        w_out,
        key_cache,
        value_cache,
        query_gain,
        key_gain,
        out_gate,
        cotangent,
    ):
        T, F = tokens.shape
        H = query_gain.shape[0]
        cached = key_cache.shape[0]
        wide_out = w_out.shape[1]
        assert w_query.shape == (k * F, H) and w_out.shape == (k * H, wide_out) and T == H
        query_gain = query_gain.reshape(1, H)
        key_gain = key_gain.reshape(1, H)
        out_gate = out_gate.reshape(1, wide_out)
        fold = H ** (-0.5) * math.log2(math.e)

        near = [s for s in range(1, R) if s & (s - 1) == 0]
        out_rows = {0: w_out, **{s: over_row(w_out, s) for s in near}}
        order = [d for d in range(R) if d.bit_count() % 2 == 0][::-1]
        mine = {d: turned(tokens, d) for d in order}
        mine.update({d ^ 1: over_z(mine[d], 1) for d in order})
        half = k * H // 2
        for s in range(1, R):
            low = s & -s
            top = s ^ low
            if top in near:
                out_rows[s] = (
                    over_row(out_rows[top][:half], low),
                    over_row(out_rows[low][half:], top),
                )
            elif top:
                out_rows[s] = (over_row(w_out, s),)

        def prepare(key_ref, value_ref, wq, wk, wv, qg, kg, key_out, value_out, weight_out, gain_out):
            key = normed(key_ref[...].astype(f32), kg[...])
            key_out[...] = key.T.astype(bf16)
            value_out[:, :H] = value_ref[...]
            value_out[:, H:] = jnp.ones((cached, H), bf16)
            weight_out[:, :H] = wq[...]
            weight_out[:, H : 2 * H] = wk[...]
            weight_out[:, 2 * H :] = wv[...]
            gain_out[0:1, :] = qg[...] * fold
            gain_out[1:2, :] = kg[...]

        keys_t, values_one, weights, gains = call(
            prepare,
            "prepare",
            (key_cache, value_cache, w_query, w_key, w_value, query_gain, key_gain),
            [
                jax.ShapeDtypeStruct((H, cached), bf16),
                jax.ShapeDtypeStruct((cached, 2 * H), bf16),
                jax.ShapeDtypeStruct((k * F, 3 * H), bf16),
                jax.ShapeDtypeStruct((2, H), f32),
            ],
            far=7,
        )

        def product(mine_refs, other_refs, weight_ref, ds):
            f, z, q = here()
            w_mine = weight_ref[pl.ds(pl.multiple_of(q * F, F), F), :]
            w_other = weight_ref[pl.ds(pl.multiple_of((1 - q) * F, F), F), :]
            mine_blocks, other_blocks = [], []
            for d, mine_ref, other_ref in zip(ds, mine_refs, other_refs):
                direct = d if d in order else d ^ 1
                crossed = jnp.logical_and(f == direct, z == d)
                a, b = mine_ref[...], other_ref[...]
                mine_blocks.append(jnp.where(crossed, b, a))
                other_blocks.append(jnp.where(crossed, a, b))
            whole_mine, whole_other = jnp.concatenate(mine_blocks), jnp.concatenate(other_blocks)
            return (dot(whole_mine, w_mine) + dot(whole_other, w_other)).astype(bf16)

        later = [d ^ 1 for d in order]
        n = len(order)

        def project_direct(*refs):
            refs[-1][...] = product(refs[:n], refs[n : 2 * n], refs[2 * n], order)

        def project(*refs):
            direct_ref, weight_ref = refs[2 * n : 2 * n + 2]
            outs, held = refs[2 * n + 2 : -1], refs[-1]
            f, z, _ = here()
            whole = product(refs[:n], refs[n : 2 * n], weight_ref, later)
            for ds, found in ((order, direct_ref), (later, whole)):
                for i, d in enumerate(ds):
                    part = found[i * T : (i + 1) * T]
                    block = f ^ z ^ d
                    rows = pl.ds(pl.multiple_of(block * T, T), T)
                    for s in range(R):
                        outs[s][rows, :] = part[:, :H]
                    held[block, :T] = part[:, H : 2 * H]
                    held[block, T:] = part[:, 2 * H :]
            for s in range(R):
                outs[s][R * T :, :] = held[f ^ s]

        direct_other = [across_chip(mine[d]) for d in order]
        (direct_part,) = call(
            project_direct,
            "project_direct",
            (*[mine[d] for d in order], *direct_other, weights),
            [jax.ShapeDtypeStruct((n * T, 3 * H), bf16)],
        )
        joined = lax.optimization_barrier(
            (
                list(mine.values()),
                [out_rows[s] for s in range(1, R)],
                [keys_t, values_one, weights, gains],
            )
        )
        slots, out_rows = dict(zip(mine, joined[0])), [w_out, *joined[1]]
        keys_t, values_one, weights, gains = joined[2]
        out_rows = [x if not isinstance(x, tuple) else x[0] if len(x) == 1 else jnp.concatenate(x) for x in out_rows]
        later_other = [across_chip(slots[d]) for d in later]
        parts = call(
            project,
            "project",
            (*[slots[d] for d in later], *later_other, direct_part, weights),
            [jax.ShapeDtypeStruct(((R + 2) * T, H), bf16)] * R,
            [pltpu.VMEM((R, 2 * T, H), bf16)],
        )
        far_first = list(range(R - 1, 0, -1))
        sent_parts = lax.optimization_barrier([over_row(parts[s], s) for s in far_first])
        parts = [parts[0], *sent_parts[::-1]]

        def gradient(*refs):
            cot_ref, gate_ref = refs[:2]
            rows_refs, outs, held = refs[2 : 2 + R], refs[2 + R : 2 + 2 * R], refs[-1]
            f, z, q = here()
            scaled = (cot_ref[...].astype(f32) * gate_ref[...]).astype(bf16)
            for s in range(R):
                part = dot_last(scaled, rows_refs[s][...]).astype(bf16)
                even, odd = part[:, :H], part[:, H:]
                held[f ^ s, :T] = jnp.where(q == 0, even, odd)
                held[f ^ s, T:] = jnp.where(q == 0, odd, even)
            for m in range(R):
                outs[m][...] = held[z ^ m]

        sent = jax.ShapeDtypeStruct((k * T, H), bf16)
        grads = call(
            gradient,
            "gradient",
            (cotangent, out_gate, *out_rows),
            [sent] * R,
            [pltpu.VMEM((R, k * T, H), bf16)],
        )
        grads = [grads[0]] + [over_z(grads[m], m) for m in range(1, R)]

        def attend(*refs):
            part_refs = refs[:R]
            keys_ref, values_ref, gain_ref = refs[R : R + 3]
            outs = refs[R + 3 : 2 * R + 3]
            query_ref, held = refs[2 * R + 3 :]
            f, _, _ = here()

            def total(rows):
                return sum(ref[rows, :].astype(f32) for ref in part_refs)

            query_ref[...] = normed(total(slice(0, R * T)), gain_ref[0:1, :]).astype(bf16)
            key_new = normed(total(slice(R * T, (R + 1) * T)), gain_ref[1:2, :]).astype(bf16)
            value_new = total(slice((R + 1) * T, (R + 2) * T)).astype(bf16)
            value_new = jnp.concatenate([value_new, jnp.ones_like(value_new)], axis=1)
            step = min(512, cached)
            eye = lax.broadcasted_iota(jnp.int32, (T, H), 0) == lax.broadcasted_iota(
                jnp.int32, (T, H), 1
            )

            def block(d, carry):
                query = query_ref[pl.ds(pl.multiple_of(d * T, T), T), :]
                weights = jnp.exp2(dot_last(query, key_new)).astype(bf16)
                sums = dot(weights, value_new)
                for j in range(0, cached, step):
                    weights = jnp.exp2(dot(query, keys_ref[:, j : j + step])).astype(bf16)
                    sums = sums + dot(weights, values_ref[j : j + step, :])
                held[d, :T] = sums[:, :H].astype(bf16)
                row = jnp.sum(jnp.where(eye, sums[:, H:], 0.0), axis=0, keepdims=True)
                high = row.astype(bf16).astype(f32)
                low = row - high
                which = lax.broadcasted_iota(jnp.int32, (tail, H), 0)
                held[d, T:] = jnp.where(which == 0, high, jnp.where(which == 1, low, 0.0)).astype(bf16)
                return carry

            lax.fori_loop(0, R, block, 0, unroll=min(R, 4))
            for s in range(R):
                outs[s][...] = held[f ^ s]

        sums = call(
            attend,
            "attend",
            (*parts, keys_t, values_one, gains),
            [jax.ShapeDtypeStruct((T + tail, H), bf16)] * R,
            [pltpu.VMEM((R * T, H), bf16), pltpu.VMEM((R, T + tail, H), bf16)],
        )
        sums = [sums[0]] + [over_row(sums[s], s) for s in range(1, R)]

        sums, grads = lax.optimization_barrier((sums, grads))

        def join(*refs):
            own_ref, away_ref = refs[R:]
            both_heads = sum(ref[...].astype(f32) for ref in refs[:R])
            own_ref[...] = both_heads[:T].astype(bf16)
            away_ref[...] = both_heads[T:].astype(bf16)

        grad_own, grad_away = call(join, "join", grads, [jax.ShapeDtypeStruct((T, H), bf16)] * 2)
        grad_away = across_chip(grad_away)

        def finish(*refs):
            sum_refs, out = refs[:R], refs[R]
            numerators = sum(ref[:T, :].astype(f32) for ref in sum_refs)
            row = sum(ref[T : T + 1, :].astype(f32) + ref[T + 1 : T + 2, :].astype(f32) for ref in sum_refs)
            eye = lax.broadcasted_iota(jnp.int32, (T, H), 0) == lax.broadcasted_iota(
                jnp.int32, (T, H), 1
            )
            totals = jnp.sum(jnp.where(eye, row, 0.0), axis=1, keepdims=True)
            out[...] = (numerators / totals).astype(bf16)

        (attention,) = call(finish, "finish", sums, [jax.ShapeDtypeStruct((T, H), bf16)])
        heads = [attention] + [over_z(attention, m) for m in range(1, R)]
        heads_other = [across_chip(x) for x in heads]

        def output(*refs):
            tokens_ref, gate_ref, own_ref, away_ref = refs[:4]
            mine_refs, other_refs, rows_refs = (refs[i * R + 4 : (i + 1) * R + 4] for i in range(3))
            layer_ref, grad_ref, held = refs[3 * R + 4 :]
            f, z, q = here()
            grad_ref[...] = (own_ref[...].astype(f32) + away_ref[...].astype(f32)).astype(bf16)
            for m in range(R):
                own, away = mine_refs[m][...], other_refs[m][...]
                held[z ^ m, :, :H] = jnp.where(q == 0, own, away)
                held[z ^ m, :, H:] = jnp.where(q == 0, away, own)
            branch = sum(dot(held[f ^ s], rows_refs[s][...]) for s in range(R))
            layer_ref[...] = (tokens_ref[...].astype(f32) + gate_ref[...] * branch).astype(bf16)

        layer_out, attention_cotangent = call(
            output,
            "output",
            (tokens, out_gate, grad_own, grad_away, *heads, *heads_other, *out_rows),
            [jax.ShapeDtypeStruct((T, wide_out), bf16), jax.ShapeDtypeStruct((T, H), bf16)],
            [pltpu.VMEM((R, T, k * H), bf16)],
        )
        return layer_out, attention_cotangent

    spread = P("row", "col")
    return jax.shard_map(
        body,
        mesh=mesh,
        in_specs=(spread,) * 7 + (P(), P(), P("col"), spread),
        out_specs=(spread, spread),
        check_vma=False,
    )
```

```python
import math

import jax
import jax.numpy as jnp
from jax import lax
from jax.experimental import pallas as pl
from jax.experimental.pallas import tpu as pltpu
from jax.sharding import PartitionSpec as P

epsilon = 1e-06
both = ("row", "col")
f32 = jnp.float32
bf16 = jnp.bfloat16
tail = 16


def size_of(arrays):
    return sum(math.prod(a.shape) * jnp.dtype(a.dtype).itemsize for a in arrays)


def call(kernel, name, operands, outs, scratch=(), far=0):
    moved = size_of(operands) + size_of(outs)
    held = moved + size_of(scratch)
    whole = pl.BlockSpec(memory_space=pltpu.VMEM)
    fetched = [pltpu.VMEM(a.shape, a.dtype) for a in operands[:far]]

    def fetch(*refs):
        n = len(operands) + len(outs)
        landed, sems = refs[n : n + far], refs[-1]
        copies = [pltpu.make_async_copy(refs[i], landed[i], sems.at[i]) for i in range(far)]
        for copy in copies:
            copy.start()
        for copy in copies:
            copy.wait()
        kernel(*landed, *refs[far:n], *refs[n + far : -1])

    return pl.pallas_call(
        fetch if far else kernel,
        out_shape=list(outs),
        in_specs=[pl.BlockSpec(memory_space=pl.ANY)] * far + [whole] * (len(operands) - far),
        out_specs=[whole] * len(outs),
        scratch_shapes=[*fetched, *scratch] + ([pltpu.SemaphoreType.DMA((far,))] if far else []),
        compiler_params=pltpu.CompilerParams(vmem_limit_bytes=2 * held + (12 << 20)),
        cost_estimate=pl.CostEstimate(flops=0, bytes_accessed=0, transcendentals=0),
        name=name,
    )(*(pltpu.with_memory_space_constraint(a, pltpu.HBM) for a in operands[:far]), *operands[far:])


def dot(a, b):
    return jnp.dot(a, b, preferred_element_type=f32)


def dot_last(a, b):
    return lax.dot_general(a, b, (((1,), (1,)), ((), ())), preferred_element_type=f32)


def normed(wide, gain):
    mean_square = jnp.mean(wide * wide, axis=-1, keepdims=True)
    return wide * lax.rsqrt(mean_square + epsilon) * gain


def solution(mesh):
    R, C = mesh.shape["row"], mesh.shape["col"]
    k = C // R
    assert C == R * k and k == 2 and R & (R - 1) == 0

    def here():
        f, c = lax.axis_index("row"), lax.axis_index("col")
        return f, c // k, c % k

    def route(to):
        return [
            (r * C + z * k + q, (lambda a, b, e: a * C + b * k + e)(*to(r, z, q)))
            for r in range(R)
            for z in range(R)
            for q in range(k)
        ]

    def across_chip(x):
        return lax.ppermute(x, both, route(lambda r, z, q: (r, z, q ^ 1)))

    def over_row(x, s):
        return lax.ppermute(x, both, route(lambda r, z, q: (r ^ s, z, q)))

    def over_z(x, m):
        return lax.ppermute(x, both, route(lambda r, z, q: (r, z ^ m, q)))

    def turned(x, d):
        return lax.ppermute(x, both, route(lambda r, z, q: (z, r ^ z ^ d, q ^ (r == z == d))))

    def body(
        tokens,
        w_query,
        w_key,
        w_value,
        w_out,
        key_cache,
        value_cache,
        query_gain,
        key_gain,
        out_gate,
        cotangent,
    ):
        T, F = tokens.shape
        H = query_gain.shape[0]
        cached = key_cache.shape[0]
        wide_out = w_out.shape[1]
        assert w_query.shape == (k * F, H) and w_out.shape == (k * H, wide_out) and T == H
        query_gain = query_gain.reshape(1, H)
        key_gain = key_gain.reshape(1, H)
        out_gate = out_gate.reshape(1, wide_out)
        fold = H ** (-0.5) * math.log2(math.e)

        near = [s for s in range(1, R) if s & (s - 1) == 0]
        out_rows = {0: w_out, **{s: over_row(w_out, s) for s in near}}
        order = [d for d in range(R) if d.bit_count() % 2 == 0][::-1]
        mine = {d: turned(tokens, d) for d in order}
        mine.update({d ^ 1: over_z(mine[d], 1) for d in order})
        half = k * H // 2
        for s in range(1, R):
            low = s & -s
            top = s ^ low
            if top in near:
                out_rows[s] = (
                    over_row(out_rows[top][:half], low),
                    over_row(out_rows[low][half:], top),
                )
            elif top:
                out_rows[s] = (over_row(w_out, s),)

        def prepare(key_ref, value_ref, wq, wk, wv, qg, kg, key_out, value_out, weight_out, gain_out):
            key = normed(key_ref[...].astype(f32), kg[...])
            key_out[...] = key.T.astype(bf16)
            value_out[:, :H] = value_ref[...]
            value_out[:, H:] = jnp.ones((cached, H), bf16)
            weight_out[:, :H] = wq[...]
            weight_out[:, H : 2 * H] = wk[...]
            weight_out[:, 2 * H :] = wv[...]
            gain_out[0:1, :] = qg[...] * fold
            gain_out[1:2, :] = kg[...]

        keys_t, values_one, weights, gains = call(
            prepare,
            "prepare",
            (key_cache, value_cache, w_query, w_key, w_value, query_gain, key_gain),
            [
                jax.ShapeDtypeStruct((H, cached), bf16),
                jax.ShapeDtypeStruct((cached, 2 * H), bf16),
                jax.ShapeDtypeStruct((k * F, 3 * H), bf16),
                jax.ShapeDtypeStruct((2, H), f32),
            ],
            far=7,
        )

        def product(mine_refs, other_refs, weight_ref, ds):
            f, z, q = here()
            w_mine = weight_ref[pl.ds(pl.multiple_of(q * F, F), F), :]
            w_other = weight_ref[pl.ds(pl.multiple_of((1 - q) * F, F), F), :]
            mine_blocks, other_blocks = [], []
            for d, mine_ref, other_ref in zip(ds, mine_refs, other_refs):
                direct = d if d in order else d ^ 1
                crossed = jnp.logical_and(f == direct, z == d)
                a, b = mine_ref[...], other_ref[...]
                mine_blocks.append(jnp.where(crossed, b, a))
                other_blocks.append(jnp.where(crossed, a, b))
            whole_mine, whole_other = jnp.concatenate(mine_blocks), jnp.concatenate(other_blocks)
            return (dot(whole_mine, w_mine) + dot(whole_other, w_other)).astype(bf16)

        later = [d ^ 1 for d in order]
        n = len(order)

        def project_direct(*refs):
            refs[-1][...] = product(refs[:n], refs[n : 2 * n], refs[2 * n], order)

        def project(*refs):
            direct_ref, weight_ref = refs[2 * n : 2 * n + 2]
            outs, held = refs[2 * n + 2 : -1], refs[-1]
            f, z, _ = here()
            whole = product(refs[:n], refs[n : 2 * n], weight_ref, later)
            for ds, found in ((order, direct_ref), (later, whole)):
                for i, d in enumerate(ds):
                    part = found[i * T : (i + 1) * T]
                    block = f ^ z ^ d
                    rows = pl.ds(pl.multiple_of(block * T, T), T)
                    for s in range(R):
                        outs[s][rows, :] = part[:, :H]
                    held[block, :T] = part[:, H : 2 * H]
                    held[block, T:] = part[:, 2 * H :]
            for s in range(R):
                outs[s][R * T :, :] = held[f ^ s]

        direct_other = [across_chip(mine[d]) for d in order]
        (direct_part,) = call(
            project_direct,
            "project_direct",
            (*[mine[d] for d in order], *direct_other, weights),
            [jax.ShapeDtypeStruct((n * T, 3 * H), bf16)],
        )
        joined = lax.optimization_barrier(
            (
                list(mine.values()),
                [out_rows[s] for s in range(1, R)],
                [keys_t, values_one, weights, gains],
            )
        )
        slots, out_rows = dict(zip(mine, joined[0])), [w_out, *joined[1]]
        keys_t, values_one, weights, gains = joined[2]
        out_rows = [x if not isinstance(x, tuple) else x[0] if len(x) == 1 else jnp.concatenate(x) for x in out_rows]
        later_other = [across_chip(slots[d]) for d in later]
        parts = call(
            project,
            "project",
            (*[slots[d] for d in later], *later_other, direct_part, weights),
            [jax.ShapeDtypeStruct(((R + 2) * T, H), bf16)] * R,
            [pltpu.VMEM((R, 2 * T, H), bf16)],
        )
        far_first = list(range(R - 1, 0, -1))
        sent_parts = lax.optimization_barrier([over_row(parts[s], s) for s in far_first])
        parts = [parts[0], *sent_parts[::-1]]

        def gradient(*refs):
            cot_ref, gate_ref = refs[:2]
            rows_refs, outs, held = refs[2 : 2 + R], refs[2 + R : 2 + 2 * R], refs[-1]
            f, z, q = here()
            scaled = (cot_ref[...].astype(f32) * gate_ref[...]).astype(bf16)
            for s in range(R):
                part = dot_last(scaled, rows_refs[s][...]).astype(bf16)
                even, odd = part[:, :H], part[:, H:]
                held[f ^ s, :T] = jnp.where(q == 0, even, odd)
                held[f ^ s, T:] = jnp.where(q == 0, odd, even)
            for m in range(R):
                outs[m][...] = held[z ^ m]

        sent = jax.ShapeDtypeStruct((k * T, H), bf16)
        grads = call(
            gradient,
            "gradient",
            (cotangent, out_gate, *out_rows),
            [sent] * R,
            [pltpu.VMEM((R, k * T, H), bf16)],
        )
        grads = [grads[0]] + [over_z(grads[m], m) for m in range(1, R)]

        def attend(*refs):
            part_refs = refs[:R]
            keys_ref, values_ref, gain_ref = refs[R : R + 3]
            outs = refs[R + 3 : 2 * R + 3]
            query_ref, held = refs[2 * R + 3 :]
            f, _, _ = here()

            def total(rows):
                return sum(ref[rows, :].astype(f32) for ref in part_refs)

            query_ref[...] = normed(total(slice(0, R * T)), gain_ref[0:1, :]).astype(bf16)
            key_new = normed(total(slice(R * T, (R + 1) * T)), gain_ref[1:2, :]).astype(bf16)
            value_new = total(slice((R + 1) * T, (R + 2) * T)).astype(bf16)
            value_new = jnp.concatenate([value_new, jnp.ones_like(value_new)], axis=1)
            step = min(512, cached)
            eye = lax.broadcasted_iota(jnp.int32, (T, H), 0) == lax.broadcasted_iota(
                jnp.int32, (T, H), 1
            )

            def block(d, carry):
                query = query_ref[pl.ds(pl.multiple_of(d * T, T), T), :]
                weights = jnp.exp2(dot_last(query, key_new)).astype(bf16)
                sums = dot(weights, value_new)
                for j in range(0, cached, step):
                    weights = jnp.exp2(dot(query, keys_ref[:, j : j + step])).astype(bf16)
                    sums = sums + dot(weights, values_ref[j : j + step, :])
                held[d, :T] = sums[:, :H].astype(bf16)
                row = jnp.sum(jnp.where(eye, sums[:, H:], 0.0), axis=0, keepdims=True)
                high = row.astype(bf16).astype(f32)
                low = row - high
                which = lax.broadcasted_iota(jnp.int32, (tail, H), 0)
                held[d, T:] = jnp.where(which == 0, high, jnp.where(which == 1, low, 0.0)).astype(bf16)
                return carry

            lax.fori_loop(0, R, block, 0, unroll=min(R, 4))
            for s in range(R):
                outs[s][...] = held[f ^ s]

        sums = call(
            attend,
            "attend",
            (*parts, keys_t, values_one, gains),
            [jax.ShapeDtypeStruct((T + tail, H), bf16)] * R,
            [pltpu.VMEM((R * T, H), bf16), pltpu.VMEM((R, T + tail, H), bf16)],
        )
        sums = [sums[0]] + [over_row(sums[s], s) for s in far_first]

        sums, grads = lax.optimization_barrier((sums, grads))

        def finish(*refs):
            sum_refs, grad_refs = refs[:R], refs[R : 2 * R]
            out, grad_own_ref, crossing_ref = refs[2 * R :]
            numerators = sum(ref[:T, :].astype(f32) for ref in sum_refs)
            row = sum(ref[T : T + 1, :].astype(f32) + ref[T + 1 : T + 2, :].astype(f32) for ref in sum_refs)
            eye = lax.broadcasted_iota(jnp.int32, (T, H), 0) == lax.broadcasted_iota(
                jnp.int32, (T, H), 1
            )
            totals = jnp.sum(jnp.where(eye, row, 0.0), axis=1, keepdims=True)
            attention = (numerators / totals).astype(bf16)
            both_heads = sum(ref[...].astype(f32) for ref in grad_refs)
            out[...] = attention
            grad_own_ref[...] = both_heads[:T].astype(bf16)
            crossing_ref[:T] = attention
            crossing_ref[T:] = both_heads[T:].astype(bf16)

        block = jax.ShapeDtypeStruct((T, H), bf16)
        attention, grad_own, crossing = call(
            finish, "finish", (*sums, *grads), [block, block, jax.ShapeDtypeStruct((2 * T, H), bf16)]
        )
        crossing = across_chip(crossing)
        heads = [attention] + [over_z(attention, m) for m in range(1, R)]
        heads_other = [crossing] + [across_chip(x) for x in heads[1:]]

        def output(*refs):
            tokens_ref, gate_ref, own_ref = refs[:3]
            mine_refs, other_refs, rows_refs = (refs[i * R + 3 : (i + 1) * R + 3] for i in range(3))
            layer_ref, grad_ref, held = refs[3 * R + 3 :]
            f, z, q = here()
            grad_ref[...] = (own_ref[...].astype(f32) + other_refs[0][T:].astype(f32)).astype(bf16)
            for m in range(R):
                own, away = mine_refs[m][...], other_refs[m][:T]
                held[z ^ m, :, :H] = jnp.where(q == 0, own, away)
                held[z ^ m, :, H:] = jnp.where(q == 0, away, own)
            branch = sum(dot(held[f ^ s], rows_refs[s][...]) for s in range(R))
            layer_ref[...] = (tokens_ref[...].astype(f32) + gate_ref[...] * branch).astype(bf16)

        layer_out, attention_cotangent = call(
            output,
            "output",
            (tokens, out_gate, grad_own, *heads, *heads_other, *out_rows),
            [jax.ShapeDtypeStruct((T, wide_out), bf16), jax.ShapeDtypeStruct((T, H), bf16)],
            [pltpu.VMEM((R, T, k * H), bf16)],
        )
        return layer_out, attention_cotangent

    spread = P("row", "col")
    return jax.shard_map(
        body,
        mesh=mesh,
        in_specs=(spread,) * 7 + (P(), P(), P("col"), spread),
        out_specs=(spread, spread),
        check_vma=False,
    )
```

```python
import math

import jax
import jax.numpy as jnp
from jax import lax
from jax.experimental import pallas as pl
from jax.experimental.pallas import tpu as pltpu
from jax.sharding import PartitionSpec as P

epsilon = 1e-06
both = ("row", "col")
f32 = jnp.float32
bf16 = jnp.bfloat16
tail = 16


def size_of(arrays):
    return sum(math.prod(a.shape) * jnp.dtype(a.dtype).itemsize for a in arrays)


def call(kernel, name, operands, outs, scratch=(), far=0):
    moved = size_of(operands) + size_of(outs)
    held = moved + size_of(scratch)
    whole = pl.BlockSpec(memory_space=pltpu.VMEM)
    fetched = [pltpu.VMEM(a.shape, a.dtype) for a in operands[:far]]

    def fetch(*refs):
        n = len(operands) + len(outs)
        landed, sems = refs[n : n + far], refs[-1]
        copies = [pltpu.make_async_copy(refs[i], landed[i], sems.at[i]) for i in range(far)]
        for copy in copies:
            copy.start()
        for copy in copies:
            copy.wait()
        kernel(*landed, *refs[far:n], *refs[n + far : -1])

    return pl.pallas_call(
        fetch if far else kernel,
        out_shape=list(outs),
        in_specs=[pl.BlockSpec(memory_space=pl.ANY)] * far + [whole] * (len(operands) - far),
        out_specs=[whole] * len(outs),
        scratch_shapes=[*fetched, *scratch] + ([pltpu.SemaphoreType.DMA((far,))] if far else []),
        compiler_params=pltpu.CompilerParams(vmem_limit_bytes=2 * held + (12 << 20)),
        cost_estimate=pl.CostEstimate(flops=0, bytes_accessed=0, transcendentals=0),
        name=name,
    )(*(pltpu.with_memory_space_constraint(a, pltpu.HBM) for a in operands[:far]), *operands[far:])


def dot(a, b):
    return jnp.dot(a, b, preferred_element_type=f32)


def dot_last(a, b):
    return lax.dot_general(a, b, (((1,), (1,)), ((), ())), preferred_element_type=f32)


def normed(wide, gain):
    mean_square = jnp.mean(wide * wide, axis=-1, keepdims=True)
    return wide * lax.rsqrt(mean_square + epsilon) * gain


def solution(mesh):
    R, C = mesh.shape["row"], mesh.shape["col"]
    k = C // R
    assert C == R * k and k == 2 and R & (R - 1) == 0

    def here():
        f, c = lax.axis_index("row"), lax.axis_index("col")
        return f, c // k, c % k

    def route(to):
        return [
            (r * C + z * k + q, (lambda a, b, e: a * C + b * k + e)(*to(r, z, q)))
            for r in range(R)
            for z in range(R)
            for q in range(k)
        ]

    def across_chip(x):
        return lax.ppermute(x, both, route(lambda r, z, q: (r, z, q ^ 1)))

    def over_row(x, s):
        return lax.ppermute(x, both, route(lambda r, z, q: (r ^ s, z, q)))

    def over_z(x, m):
        return lax.ppermute(x, both, route(lambda r, z, q: (r, z ^ m, q)))

    def turned(x, d):
        return lax.ppermute(x, both, route(lambda r, z, q: (z, r ^ z ^ d, q ^ (r == z == d))))

    def body(
        tokens,
        w_query,
        w_key,
        w_value,
        w_out,
        key_cache,
        value_cache,
        query_gain,
        key_gain,
        out_gate,
        cotangent,
    ):
        T, F = tokens.shape
        H = query_gain.shape[0]
        cached = key_cache.shape[0]
        wide_out = w_out.shape[1]
        assert w_query.shape == (k * F, H) and w_out.shape == (k * H, wide_out) and T == H
        query_gain = query_gain.reshape(1, H)
        key_gain = key_gain.reshape(1, H)
        out_gate = out_gate.reshape(1, wide_out)
        fold = H ** (-0.5) * math.log2(math.e)

        near = [s for s in range(1, R) if s & (s - 1) == 0]
        out_rows = {0: w_out, **{s: over_row(w_out, s) for s in near}}
        order = [d for d in range(R) if d.bit_count() % 2 == 0][::-1]
        mine = {d: turned(tokens, d) for d in order}
        mine.update({d ^ 1: over_z(mine[d], 1) for d in order})
        half = k * H // 2
        for s in range(1, R):
            low = s & -s
            top = s ^ low
            if top in near:
                out_rows[s] = (
                    over_row(out_rows[top][:half], low),
                    over_row(out_rows[low][half:], top),
                )
            elif top:
                out_rows[s] = (over_row(w_out, s),)

        def prepare(key_ref, value_ref, wq, wk, wv, qg, kg, key_out, value_out, weight_out, gain_out):
            key = normed(key_ref[...].astype(f32), kg[...])
            key_out[...] = key.T.astype(bf16)
            value_out[:, :H] = value_ref[...]
            value_out[:, H:] = jnp.ones((cached, H), bf16)
            weight_out[:, :H] = wq[...]
            weight_out[:, H : 2 * H] = wk[...]
            weight_out[:, 2 * H :] = wv[...]
            gain_out[0:1, :] = qg[...] * fold
            gain_out[1:2, :] = kg[...]

        keys_t, values_one, weights, gains = call(
            prepare,
            "prepare",
            (key_cache, value_cache, w_query, w_key, w_value, query_gain, key_gain),
            [
                jax.ShapeDtypeStruct((H, cached), bf16),
                jax.ShapeDtypeStruct((cached, 2 * H), bf16),
                jax.ShapeDtypeStruct((k * F, 3 * H), bf16),
                jax.ShapeDtypeStruct((2, H), f32),
            ],
            far=7,
        )

        def product(mine_refs, other_refs, weight_ref, ds):
            f, z, q = here()
            w_mine = weight_ref[pl.ds(pl.multiple_of(q * F, F), F), :]
            w_other = weight_ref[pl.ds(pl.multiple_of((1 - q) * F, F), F), :]
            mine_blocks, other_blocks = [], []
            for d, mine_ref, other_ref in zip(ds, mine_refs, other_refs):
                direct = d if d in order else d ^ 1
                crossed = jnp.logical_and(f == direct, z == d)
                a, b = mine_ref[...], other_ref[...]
                mine_blocks.append(jnp.where(crossed, b, a))
                other_blocks.append(jnp.where(crossed, a, b))
            whole_mine, whole_other = jnp.concatenate(mine_blocks), jnp.concatenate(other_blocks)
            return (dot(whole_mine, w_mine) + dot(whole_other, w_other)).astype(bf16)

        later = [d ^ 1 for d in order]
        n = len(order)

        def project_direct(*refs):
            refs[-1][...] = product(refs[:n], refs[n : 2 * n], refs[2 * n], order)

        def project(*refs):
            direct_ref, weight_ref = refs[2 * n : 2 * n + 2]
            outs, held = refs[2 * n + 2 : -1], refs[-1]
            f, z, _ = here()
            whole = product(refs[:n], refs[n : 2 * n], weight_ref, later)
            for ds, found in ((order, direct_ref), (later, whole)):
                for i, d in enumerate(ds):
                    part = found[i * T : (i + 1) * T]
                    block = f ^ z ^ d
                    rows = pl.ds(pl.multiple_of(block * T, T), T)
                    for s in range(R):
                        outs[s][rows, :] = part[:, :H]
                    held[block, :T] = part[:, H : 2 * H]
                    held[block, T:] = part[:, 2 * H :]
            for s in range(R):
                outs[s][R * T :, :] = held[f ^ s]

        direct_other = [across_chip(x) for x in lax.optimization_barrier([mine[d] for d in order])]
        (direct_part,) = call(
            project_direct,
            "project_direct",
            (*[mine[d] for d in order], *direct_other, weights),
            [jax.ShapeDtypeStruct((n * T, 3 * H), bf16)],
        )
        joined = lax.optimization_barrier(
            (
                list(mine.values()),
                [out_rows[s] for s in range(1, R)],
                [keys_t, values_one, weights, gains],
            )
        )
        slots, out_rows = dict(zip(mine, joined[0])), [w_out, *joined[1]]
        keys_t, values_one, weights, gains = joined[2]
        out_rows = [x if not isinstance(x, tuple) else x[0] if len(x) == 1 else jnp.concatenate(x) for x in out_rows]
        later_other = [across_chip(slots[d]) for d in later]
        parts = call(
            project,
            "project",
            (*[slots[d] for d in later], *later_other, direct_part, weights),
            [jax.ShapeDtypeStruct(((R + 2) * T, H), bf16)] * R,
            [pltpu.VMEM((R, 2 * T, H), bf16)],
        )
        far_first = list(range(R - 1, 0, -1))
        sent_parts = lax.optimization_barrier([over_row(parts[s], s) for s in far_first])
        parts = [parts[0], *sent_parts[::-1]]

        def gradient(*refs):
            cot_ref, gate_ref = refs[:2]
            rows_refs, outs, held = refs[2 : 2 + R], refs[2 + R : 2 + 2 * R], refs[-1]
            f, z, q = here()
            scaled = (cot_ref[...].astype(f32) * gate_ref[...]).astype(bf16)
            for s in range(R):
                part = dot_last(scaled, rows_refs[s][...]).astype(bf16)
                even, odd = part[:, :H], part[:, H:]
                held[f ^ s, :T] = jnp.where(q == 0, even, odd)
                held[f ^ s, T:] = jnp.where(q == 0, odd, even)
            for m in range(R):
                outs[m][...] = held[z ^ m]

        sent = jax.ShapeDtypeStruct((k * T, H), bf16)
        grads = call(
            gradient,
            "gradient",
            (cotangent, out_gate, *out_rows),
            [sent] * R,
            [pltpu.VMEM((R, k * T, H), bf16)],
        )
        grads = [grads[0]] + [over_z(grads[m], m) for m in range(1, R)]

        def attend(*refs):
            part_refs = refs[:R]
            keys_ref, values_ref, gain_ref = refs[R : R + 3]
            outs = refs[R + 3 : 2 * R + 3]
            query_ref, held = refs[2 * R + 3 :]
            f, _, _ = here()

            def total(rows):
                return sum(ref[rows, :].astype(f32) for ref in part_refs)

            query_ref[...] = normed(total(slice(0, R * T)), gain_ref[0:1, :]).astype(bf16)
            key_new = normed(total(slice(R * T, (R + 1) * T)), gain_ref[1:2, :]).astype(bf16)
            value_new = total(slice((R + 1) * T, (R + 2) * T)).astype(bf16)
            value_new = jnp.concatenate([value_new, jnp.ones_like(value_new)], axis=1)
            step = min(512, cached)
            eye = lax.broadcasted_iota(jnp.int32, (T, H), 0) == lax.broadcasted_iota(
                jnp.int32, (T, H), 1
            )

            def block(d, carry):
                query = query_ref[pl.ds(pl.multiple_of(d * T, T), T), :]
                weights = jnp.exp2(dot_last(query, key_new)).astype(bf16)
                sums = dot(weights, value_new)
                for j in range(0, cached, step):
                    weights = jnp.exp2(dot(query, keys_ref[:, j : j + step])).astype(bf16)
                    sums = sums + dot(weights, values_ref[j : j + step, :])
                held[d, :T] = sums[:, :H].astype(bf16)
                row = jnp.sum(jnp.where(eye, sums[:, H:], 0.0), axis=0, keepdims=True)
                high = row.astype(bf16).astype(f32)
                low = row - high
                which = lax.broadcasted_iota(jnp.int32, (tail, H), 0)
                held[d, T:] = jnp.where(which == 0, high, jnp.where(which == 1, low, 0.0)).astype(bf16)
                return carry

            lax.fori_loop(0, R, block, 0, unroll=min(R, 4))
            for s in range(R):
                outs[s][...] = held[f ^ s]

        sums = call(
            attend,
            "attend",
            (*parts, keys_t, values_one, gains),
            [jax.ShapeDtypeStruct((T + tail, H), bf16)] * R,
            [pltpu.VMEM((R * T, H), bf16), pltpu.VMEM((R, T + tail, H), bf16)],
        )
        sums = [sums[0]] + [over_row(sums[s], s) for s in far_first]

        sums, grads = lax.optimization_barrier((sums, grads))

        def finish(*refs):
            sum_refs, grad_refs = refs[:R], refs[R : 2 * R]
            out, grad_own_ref, crossing_ref = refs[2 * R :]
            numerators = sum(ref[:T, :].astype(f32) for ref in sum_refs)
            row = sum(ref[T : T + 1, :].astype(f32) + ref[T + 1 : T + 2, :].astype(f32) for ref in sum_refs)
            eye = lax.broadcasted_iota(jnp.int32, (T, H), 0) == lax.broadcasted_iota(
                jnp.int32, (T, H), 1
            )
            totals = jnp.sum(jnp.where(eye, row, 0.0), axis=1, keepdims=True)
            attention = (numerators / totals).astype(bf16)
            both_heads = sum(ref[...].astype(f32) for ref in grad_refs)
            out[...] = attention
            grad_own_ref[...] = both_heads[:T].astype(bf16)
            crossing_ref[:T] = attention
            crossing_ref[T:] = both_heads[T:].astype(bf16)

        block = jax.ShapeDtypeStruct((T, H), bf16)
        attention, grad_own, crossing = call(
            finish, "finish", (*sums, *grads), [block, block, jax.ShapeDtypeStruct((2 * T, H), bf16)]
        )
        crossing = across_chip(crossing)
        heads = [attention] + [over_z(attention, m) for m in range(1, R)]
        heads_other = [crossing] + [across_chip(x) for x in heads[1:]]

        def output(*refs):
            tokens_ref, gate_ref, own_ref = refs[:3]
            mine_refs, other_refs, rows_refs = (refs[i * R + 3 : (i + 1) * R + 3] for i in range(3))
            layer_ref, grad_ref, held = refs[3 * R + 3 :]
            f, z, q = here()
            grad_ref[...] = (own_ref[...].astype(f32) + other_refs[0][T:].astype(f32)).astype(bf16)
            for m in range(R):
                own, away = mine_refs[m][...], other_refs[m][:T]
                held[z ^ m, :, :H] = jnp.where(q == 0, own, away)
                held[z ^ m, :, H:] = jnp.where(q == 0, away, own)
            branch = sum(dot(held[f ^ s], rows_refs[s][...]) for s in range(R))
            layer_ref[...] = (tokens_ref[...].astype(f32) + gate_ref[...] * branch).astype(bf16)

        layer_out, attention_cotangent = call(
            output,
            "output",
            (tokens, out_gate, grad_own, *heads, *heads_other, *out_rows),
            [jax.ShapeDtypeStruct((T, wide_out), bf16), jax.ShapeDtypeStruct((T, H), bf16)],
            [pltpu.VMEM((R, T, k * H), bf16)],
        )
        return layer_out, attention_cotangent

    spread = P("row", "col")
    return jax.shard_map(
        body,
        mesh=mesh,
        in_specs=(spread,) * 7 + (P(), P(), P("col"), spread),
        out_specs=(spread, spread),
        check_vma=False,
    )
```

```python
import math

import jax
import jax.numpy as jnp
from jax import lax
from jax.experimental import pallas as pl
from jax.experimental.pallas import tpu as pltpu
from jax.sharding import PartitionSpec as P

epsilon = 1e-06
both = ("row", "col")
f32 = jnp.float32
bf16 = jnp.bfloat16
tail = 16


def size_of(arrays):
    return sum(math.prod(a.shape) * jnp.dtype(a.dtype).itemsize for a in arrays)


def call(kernel, name, operands, outs, scratch=(), far=0):
    moved = size_of(operands) + size_of(outs)
    held = moved + size_of(scratch)
    whole = pl.BlockSpec(memory_space=pltpu.VMEM)
    fetched = [pltpu.VMEM(a.shape, a.dtype) for a in operands[:far]]

    def fetch(*refs):
        n = len(operands) + len(outs)
        landed, sems = refs[n : n + far], refs[-1]
        copies = [pltpu.make_async_copy(refs[i], landed[i], sems.at[i]) for i in range(far)]
        for copy in copies:
            copy.start()
        for copy in copies:
            copy.wait()
        kernel(*landed, *refs[far:n], *refs[n + far : -1])

    return pl.pallas_call(
        fetch if far else kernel,
        out_shape=list(outs),
        in_specs=[pl.BlockSpec(memory_space=pl.ANY)] * far + [whole] * (len(operands) - far),
        out_specs=[whole] * len(outs),
        scratch_shapes=[*fetched, *scratch] + ([pltpu.SemaphoreType.DMA((far,))] if far else []),
        compiler_params=pltpu.CompilerParams(vmem_limit_bytes=2 * held + (12 << 20)),
        cost_estimate=pl.CostEstimate(flops=0, bytes_accessed=0, transcendentals=0),
        name=name,
    )(*(pltpu.with_memory_space_constraint(a, pltpu.HBM) for a in operands[:far]), *operands[far:])


def dot(a, b):
    return jnp.dot(a, b, preferred_element_type=f32)


def dot_last(a, b):
    return lax.dot_general(a, b, (((1,), (1,)), ((), ())), preferred_element_type=f32)


def normed(wide, gain):
    mean_square = jnp.mean(wide * wide, axis=-1, keepdims=True)
    return wide * lax.rsqrt(mean_square + epsilon) * gain


def solution(mesh):
    R, C = mesh.shape["row"], mesh.shape["col"]
    k = C // R
    assert C == R * k and k == 2 and R & (R - 1) == 0

    def here():
        f, c = lax.axis_index("row"), lax.axis_index("col")
        return f, c // k, c % k

    def route(to):
        return [
            (r * C + z * k + q, (lambda a, b, e: a * C + b * k + e)(*to(r, z, q)))
            for r in range(R)
            for z in range(R)
            for q in range(k)
        ]

    def across_chip(x):
        return lax.ppermute(x, both, route(lambda r, z, q: (r, z, q ^ 1)))

    def over_row(x, s):
        return lax.ppermute(x, both, route(lambda r, z, q: (r ^ s, z, q)))

    def over_z(x, m):
        return lax.ppermute(x, both, route(lambda r, z, q: (r, z ^ m, q)))

    def turned(x, d):
        return lax.ppermute(x, both, route(lambda r, z, q: (z, r ^ z ^ d, q ^ (r == z == d))))

    def body(
        tokens,
        w_query,
        w_key,
        w_value,
        w_out,
        key_cache,
        value_cache,
        query_gain,
        key_gain,
        out_gate,
        cotangent,
    ):
        T, F = tokens.shape
        H = query_gain.shape[0]
        cached = key_cache.shape[0]
        wide_out = w_out.shape[1]
        assert w_query.shape == (k * F, H) and w_out.shape == (k * H, wide_out) and T == H
        query_gain = query_gain.reshape(1, H)
        key_gain = key_gain.reshape(1, H)
        out_gate = out_gate.reshape(1, wide_out)
        fold = H ** (-0.5) * math.log2(math.e)

        near = [s for s in range(1, R) if s & (s - 1) == 0]
        out_rows = {0: w_out, **{s: over_row(w_out, s) for s in near}}
        order = [d for d in range(R) if d.bit_count() % 2 == 0][::-1]
        mine = {d: turned(tokens, d) for d in order}
        mine.update({d ^ 1: over_z(mine[d], 1) for d in order})
        half = k * H // 2
        for s in range(1, R):
            low = s & -s
            top = s ^ low
            if top in near:
                out_rows[s] = (
                    over_row(out_rows[top][:half], low),
                    over_row(out_rows[low][half:], top),
                )
            elif top:
                out_rows[s] = (over_row(w_out, s),)

        def prepare(key_ref, value_ref, wq, wk, wv, qg, kg, key_out, value_out, weight_out, gain_out):
            key = normed(key_ref[...].astype(f32), kg[...])
            key_out[...] = key.T.astype(bf16)
            value_out[:, :H] = value_ref[...]
            value_out[:, H:] = jnp.ones((cached, H), bf16)
            weight_out[:, :H] = wq[...]
            weight_out[:, H : 2 * H] = wk[...]
            weight_out[:, 2 * H :] = wv[...]
            gain_out[0:1, :] = qg[...] * fold
            gain_out[1:2, :] = kg[...]

        keys_t, values_one, weights, gains = call(
            prepare,
            "prepare",
            (key_cache, value_cache, w_query, w_key, w_value, query_gain, key_gain),
            [
                jax.ShapeDtypeStruct((H, cached), bf16),
                jax.ShapeDtypeStruct((cached, 2 * H), bf16),
                jax.ShapeDtypeStruct((k * F, 3 * H), bf16),
                jax.ShapeDtypeStruct((2, H), f32),
            ],
            far=7,
        )

        def product(mine_refs, other_refs, weight_ref, ds):
            f, z, q = here()
            w_mine = weight_ref[pl.ds(pl.multiple_of(q * F, F), F), :]
            w_other = weight_ref[pl.ds(pl.multiple_of((1 - q) * F, F), F), :]
            mine_blocks, other_blocks = [], []
            for d, mine_ref, other_ref in zip(ds, mine_refs, other_refs):
                direct = d if d in order else d ^ 1
                crossed = jnp.logical_and(f == direct, z == d)
                a, b = mine_ref[...], other_ref[...]
                mine_blocks.append(jnp.where(crossed, b, a))
                other_blocks.append(jnp.where(crossed, a, b))
            whole_mine, whole_other = jnp.concatenate(mine_blocks), jnp.concatenate(other_blocks)
            return (dot(whole_mine, w_mine) + dot(whole_other, w_other)).astype(bf16)

        later = [d ^ 1 for d in order]
        n = len(order)

        def project_direct(*refs):
            refs[-1][...] = product(refs[:n], refs[n : 2 * n], refs[2 * n], order)

        def project(*refs):
            direct_ref, weight_ref = refs[2 * n : 2 * n + 2]
            outs, held = refs[2 * n + 2 : -1], refs[-1]
            f, z, _ = here()
            whole = product(refs[:n], refs[n : 2 * n], weight_ref, later)
            for ds, found in ((order, direct_ref), (later, whole)):
                for i, d in enumerate(ds):
                    part = found[i * T : (i + 1) * T]
                    block = f ^ z ^ d
                    rows = pl.ds(pl.multiple_of(block * T, T), T)
                    for s in range(R):
                        outs[s][rows, :] = part[:, :H]
                    held[block, :T] = part[:, H : 2 * H]
                    held[block, T:] = part[:, 2 * H :]
            for s in range(R):
                outs[s][R * T :, :] = held[f ^ s]

        direct_other = [across_chip(x) for x in lax.optimization_barrier([mine[d] for d in order])]
        (direct_part,) = call(
            project_direct,
            "project_direct",
            (*[mine[d] for d in order], *direct_other, weights),
            [jax.ShapeDtypeStruct((n * T, 3 * H), bf16)],
        )
        joined = lax.optimization_barrier(
            (
                list(mine.values()),
                [out_rows[s] for s in range(1, R)],
                [keys_t, values_one, weights, gains],
            )
        )
        slots, out_rows = dict(zip(mine, joined[0])), [w_out, *joined[1]]
        keys_t, values_one, weights, gains = joined[2]
        out_rows = [x if not isinstance(x, tuple) else x[0] if len(x) == 1 else jnp.concatenate(x) for x in out_rows]
        later_other = [across_chip(slots[d]) for d in later]
        parts = call(
            project,
            "project",
            (*[slots[d] for d in later], *later_other, direct_part, weights),
            [jax.ShapeDtypeStruct(((R + 2) * T, H), bf16)] * R,
            [pltpu.VMEM((R, 2 * T, H), bf16)],
        )
        far_first = list(range(R - 1, 0, -1))
        sent_parts = lax.optimization_barrier([over_row(parts[s], s) for s in far_first])
        parts = [parts[0], *sent_parts[::-1]]

        def gradient(*refs):
            cot_ref, gate_ref = refs[:2]
            rows_refs, outs, held = refs[2 : 2 + R], refs[2 + R : 2 + 2 * R], refs[-1]
            f, z, q = here()
            scaled = (cot_ref[...].astype(f32) * gate_ref[...]).astype(bf16)
            for s in range(R):
                part = dot_last(scaled, rows_refs[s][...]).astype(bf16)
                even, odd = part[:, :H], part[:, H:]
                held[f ^ s, :T] = jnp.where(q == 0, even, odd)
                held[f ^ s, T:] = jnp.where(q == 0, odd, even)
            for m in range(R):
                outs[m][...] = held[z ^ m]

        sent = jax.ShapeDtypeStruct((k * T, H), bf16)
        grads = call(
            gradient,
            "gradient",
            (cotangent, out_gate, *out_rows),
            [sent] * R,
            [pltpu.VMEM((R, k * T, H), bf16)],
        )
        grads = [grads[0]] + [over_z(grads[m], m) for m in range(1, R)]

        def attend(*refs):
            part_refs = refs[:R]
            keys_ref, values_ref, gain_ref = refs[R : R + 3]
            outs = refs[R + 3 : 2 * R + 3]
            query_ref, held = refs[2 * R + 3 :]
            f, _, _ = here()

            def total(rows):
                return sum(ref[rows, :].astype(f32) for ref in part_refs)

            query_ref[...] = normed(total(slice(0, R * T)), gain_ref[0:1, :]).astype(bf16)
            key_new = normed(total(slice(R * T, (R + 1) * T)), gain_ref[1:2, :]).astype(bf16)
            value_new = total(slice((R + 1) * T, (R + 2) * T)).astype(bf16)
            value_new = jnp.concatenate([value_new, jnp.ones_like(value_new)], axis=1)
            step = min(2048, cached)
            eye = lax.broadcasted_iota(jnp.int32, (T, H), 0) == lax.broadcasted_iota(
                jnp.int32, (T, H), 1
            )

            def block(d, carry):
                query = query_ref[pl.ds(pl.multiple_of(d * T, T), T), :]
                weights = jnp.exp2(dot_last(query, key_new)).astype(bf16)
                sums = dot(weights, value_new)
                for j in range(0, cached, step):
                    weights = jnp.exp2(dot(query, keys_ref[:, j : j + step])).astype(bf16)
                    sums = sums + dot(weights, values_ref[j : j + step, :])
                held[d, :T] = sums[:, :H].astype(bf16)
                row = jnp.sum(jnp.where(eye, sums[:, H:], 0.0), axis=0, keepdims=True)
                high = row.astype(bf16).astype(f32)
                low = row - high
                which = lax.broadcasted_iota(jnp.int32, (tail, H), 0)
                held[d, T:] = jnp.where(which == 0, high, jnp.where(which == 1, low, 0.0)).astype(bf16)
                return carry

            lax.fori_loop(0, R, block, 0, unroll=min(R, 4))
            for s in range(R):
                outs[s][...] = held[f ^ s]

        sums = call(
            attend,
            "attend",
            (*parts, keys_t, values_one, gains),
            [jax.ShapeDtypeStruct((T + tail, H), bf16)] * R,
            [pltpu.VMEM((R * T, H), bf16), pltpu.VMEM((R, T + tail, H), bf16)],
        )
        sums = [sums[0]] + [over_row(sums[s], s) for s in far_first]

        sums, grads = lax.optimization_barrier((sums, grads))

        def finish(*refs):
            sum_refs, grad_refs = refs[:R], refs[R : 2 * R]
            out, grad_own_ref, crossing_ref = refs[2 * R :]
            numerators = sum(ref[:T, :].astype(f32) for ref in sum_refs)
            row = sum(ref[T : T + 1, :].astype(f32) + ref[T + 1 : T + 2, :].astype(f32) for ref in sum_refs)
            eye = lax.broadcasted_iota(jnp.int32, (T, H), 0) == lax.broadcasted_iota(
                jnp.int32, (T, H), 1
            )
            totals = jnp.sum(jnp.where(eye, row, 0.0), axis=1, keepdims=True)
            attention = (numerators / totals).astype(bf16)
            both_heads = sum(ref[...].astype(f32) for ref in grad_refs)
            out[...] = attention
            grad_own_ref[...] = both_heads[:T].astype(bf16)
            crossing_ref[:T] = attention
            crossing_ref[T:] = both_heads[T:].astype(bf16)

        block = jax.ShapeDtypeStruct((T, H), bf16)
        attention, grad_own, crossing = call(
            finish, "finish", (*sums, *grads), [block, block, jax.ShapeDtypeStruct((2 * T, H), bf16)]
        )
        crossing = across_chip(crossing)
        heads = [attention] + [over_z(attention, m) for m in range(1, R)]
        heads_other = [crossing] + [across_chip(x) for x in heads[1:]]

        def output(*refs):
            tokens_ref, gate_ref, own_ref = refs[:3]
            mine_refs, other_refs, rows_refs = (refs[i * R + 3 : (i + 1) * R + 3] for i in range(3))
            layer_ref, grad_ref, held = refs[3 * R + 3 :]
            f, z, q = here()
            grad_ref[...] = (own_ref[...].astype(f32) + other_refs[0][T:].astype(f32)).astype(bf16)
            for m in range(R):
                own, away = mine_refs[m][...], other_refs[m][:T]
                held[z ^ m, :, :H] = jnp.where(q == 0, own, away)
                held[z ^ m, :, H:] = jnp.where(q == 0, away, own)
            branch = sum(dot(held[f ^ s], rows_refs[s][...]) for s in range(R))
            layer_ref[...] = (tokens_ref[...].astype(f32) + gate_ref[...] * branch).astype(bf16)

        layer_out, attention_cotangent = call(
            output,
            "output",
            (tokens, out_gate, grad_own, *heads, *heads_other, *out_rows),
            [jax.ShapeDtypeStruct((T, wide_out), bf16), jax.ShapeDtypeStruct((T, H), bf16)],
            [pltpu.VMEM((R, T, k * H), bf16)],
        )
        return layer_out, attention_cotangent

    spread = P("row", "col")
    return jax.shard_map(
        body,
        mesh=mesh,
        in_specs=(spread,) * 7 + (P(), P(), P("col"), spread),
        out_specs=(spread, spread),
        check_vma=False,
    )
```
